512 devices in a mesh: day: 16 (over z, x_lo), sta: 32 (over y, x_hi, core).
Axes of the slice: x: 4 (x_hi: 2, x_lo: 2; x = x_hi * 2 + x_lo), y: 8, z: 8, core: 2. Of those that a mesh axis runs over, the one named last changes fastest.
Arguments:
- record: bfloat16 [64, 256, 1024], P('day', 'sta'), may hold values from -6 to 6
- alive_mask: int32 [64, 256], replicated, may hold values from 0 to 1
- owners: int32 [4], replicated, may hold values from 0 to 31, as said below
Outputs:
- stacks: float32 [256, 32, 257], P('sta', 'day')
The draws below stay inside these ranges and needn't reach their ends.
Inputs may be any that keep to these rules, and one draw needn't show every extreme that they name: `owners`: 4 distinct indices of the sta axis, among them always the first and the last.
All inputs are finite; a program needn't handle non-finite values.
Results may differ from the reference program's by a relative error of at most 0.005.
Values may be sent and summed in bfloat16 or wider, within the bound.
No kernel may reach another device: no remote copies, remote signals or barrier semaphores. Data moves between devices by JAX's collectives and lax.ppermute only.
A program may use at most 128 MiB of HBM per device.

```python
import math
import jax
import jax.numpy as jnp
from jax import lax

NSAMP = 1024
MAXLAG = 128
OWNERS = 4
STA_DEV = 8
W_DEV = 4
FREQ = 512
LAGS = 257
STATIONS = 256
WINDOWS = 64
SOURCES = 32
N_DAY = 16
N_STA = 32


def draw_alive_mask(key, part):
    key = jax.random.fold_in(key, 11)
    dead_key, live_key = jax.random.split(key)
    dead_draw = jax.random.randint(dead_key, (STATIONS,), 0, 8)
    living = jax.random.randint(live_key, (WINDOWS, STATIONS), 0, 4)
    return jnp.where((dead_draw[None, :] > 0) & (living > 0), 1, 0).astype(jnp.int32)


def draw_owners(key, part):
    key = jax.random.fold_in(key, 23)
    middle_key, order_key = jax.random.split(key)
    middle = (jax.random.permutation(middle_key, N_STA - 2) + 1).astype(jnp.int32)
    ends = jnp.array([0, N_STA - 1], dtype=jnp.int32)
    picked = jnp.concatenate([ends, middle[:OWNERS - 2]], axis=0)
    order = jax.random.permutation(order_key, OWNERS)
    return picked[order].astype(jnp.int32)


def block_scale(own_key, extent, pieces, low, top_value):
    gain, own = 1.0, jax.random.fold_in(own_key, 6)
    for dim, blocks in pieces:
        steps = jnp.exp(jax.random.uniform(jax.random.fold_in(own, dim), (blocks,), jnp.float32, low / len(pieces), top_value / len(pieces)))
        gain = gain * jnp.repeat(steps, extent[dim] // blocks).reshape([-1 if axis == dim else 1 for axis in range(len(extent))])
    return gain


def scatter_about(rng, dims, spread, bound, pieces=(), kind=jnp.bfloat16):
    factor_of = block_scale(rng, dims, pieces, -0.22, 0.18) if pieces else 1.0
    values = jax.random.normal(rng, dims, jnp.float32) * spread * factor_of
    return jnp.minimum(jnp.maximum(values, -bound), bound).astype(kind)


def setup_inputs(seed: int = 0) -> dict:
    splits = jax.random.split(jax.random.key(seed), 4)
    record = scatter_about(splits[0], (WINDOWS, STATIONS, NSAMP), 1.0, 6.0, ((0, 16), (1, 32)))
    alive_mask = draw_alive_mask(jax.random.fold_in(splits[3], 71), 0)
    owners = draw_owners(jax.random.fold_in(splits[3], 71), 0)
    return {"record": record, "alive_mask": alive_mask, "owners": owners}


def forward_table(samples, half_len):
    times = jnp.arange(samples, dtype=jnp.int32)[:, None]
    bins = jnp.arange(1, half_len + 1, dtype=jnp.int32)[None, :]
    phase = (times * bins % samples).astype(jnp.float32) * (2.0 * math.pi / samples)
    return jnp.concatenate([jnp.cos(phase).astype(jnp.bfloat16), (-jnp.sin(phase)).astype(jnp.bfloat16)], axis=1)

def lag_table(samples, half_len, reach):
    bins = jnp.arange(1, half_len + 1, dtype=jnp.int32)[:, None]
    shifts = jnp.arange(-reach, reach + 1, dtype=jnp.int32)[None, :]
    phase = (bins * shifts % samples).astype(jnp.float32) * (2.0 * math.pi / samples)
    weight = jnp.where(bins == half_len, 1.0, 2.0).astype(jnp.float32) / math.sqrt(samples)
    return jnp.concatenate([weight * jnp.cos(phase), -weight * jnp.sin(phase)], axis=0).astype(jnp.bfloat16)

def whiten(record, mask_real, forward):
    windows, stations, samples = record.shape
    half_len = forward.shape[1] // 2
    spectrum = jnp.dot(record.reshape(-1, samples).astype(jnp.float32), forward.astype(jnp.float32), precision=lax.Precision.HIGHEST)
    spectrum = spectrum.reshape(windows, stations, 2 * half_len)
    real_part = spectrum[..., :half_len]
    imag_part = spectrum[..., half_len:]
    magnitude = jnp.sqrt(real_part * real_part + imag_part * imag_part)
    level = lax.optimization_barrier(jnp.mean(magnitude, axis=-1, keepdims=True))
    factor = mask_real[..., None] / (magnitude + 0.3 * level + 1e-06)
    return jnp.concatenate([real_part * factor, imag_part * factor], axis=-1).astype(jnp.bfloat16)

def reference(record, alive_mask, owners):
    forward = forward_table(NSAMP, FREQ)
    lag_rows = lag_table(NSAMP, FREQ, MAXLAG).astype(jnp.float32)
    mask_real = alive_mask.astype(jnp.float32)
    whitened = whiten(record, mask_real, forward)
    source_index = (owners[:, None] * STA_DEV + jnp.arange(STA_DEV, dtype=jnp.int32)[None, :]).reshape(-1).astype(jnp.int32)
    source_white = jnp.take(whitened, source_index, axis=1)
    source_mask = jnp.take(mask_real, source_index, axis=1)
    source_group = source_white.reshape(N_DAY, W_DEV, SOURCES, NSAMP).astype(jnp.float32)
    src_real = source_group[..., :FREQ]
    src_imag = source_group[..., FREQ:]
    highest = lax.Precision.HIGHEST

    def one_block(block_pos):
        first_col = (block_pos * STA_DEV).astype(jnp.int32)
        own_block = lax.dynamic_slice_in_dim(whitened, first_col, STA_DEV, 1)
        own_block = own_block.reshape(N_DAY, W_DEV, STA_DEV, NSAMP).astype(jnp.float32)
        own_real = own_block[..., :FREQ]
        own_imag = own_block[..., FREQ:]
        cross_real = jnp.einsum('gwmf,gwof->gmof', own_real, src_real, precision=highest) + jnp.einsum('gwmf,gwof->gmof', own_imag, src_imag, precision=highest)
        cross_imag = jnp.einsum('gwmf,gwof->gmof', own_imag, src_real, precision=highest) - jnp.einsum('gwmf,gwof->gmof', own_real, src_imag, precision=highest)
        cross = jnp.concatenate([cross_real, cross_imag], axis=-1).astype(jnp.bfloat16)
        cross = lax.optimization_barrier(cross).astype(jnp.float32)
        summed = lax.optimization_barrier(jnp.sum(cross, axis=0))
        correlation = jnp.einsum('mok,kl->mol', summed, lag_rows, precision=highest)
        own_mask = lax.dynamic_slice_in_dim(mask_real, first_col, STA_DEV, 1)
        counts = jnp.dot(own_mask.T, source_mask, precision=highest)
        return correlation / jnp.sqrt(jnp.maximum(counts, 1.0))[..., None]
    stacks = lax.map(one_block, jnp.arange(N_STA, dtype=jnp.int32))
    return stacks.reshape(STATIONS, SOURCES, LAGS)
```

```python
import math

import jax
import jax.numpy as jnp
import numpy as np
from jax import lax
from jax.experimental import pallas as pl
from jax.experimental.pallas import tpu as pltpu
from jax.sharding import PartitionSpec as P

MAXLAG = 128
OWNERS = 4
LANES = 384
SHARE = 4


def forward_table(samples, half_len):
    times = np.arange(samples)[:, None]
    bins = np.arange(1, half_len + 1)[None, :]
    phase = (times * bins % samples).astype(np.float32) * np.float32(2.0 * math.pi / samples)
    return np.concatenate([np.cos(phase), -np.sin(phase)], axis=1).astype(jnp.bfloat16)


def lag_table(samples, half_len, reach):
    bins = np.arange(1, half_len + 1)[:, None]
    shifts = np.arange(-reach, reach + 1)[None, :]
    phase = (bins * shifts % samples).astype(np.float32) * np.float32(2.0 * math.pi / samples)
    weight = (np.where(bins == half_len, 1.0, 2.0) / math.sqrt(samples)).astype(np.float32)
    table = np.concatenate([weight * np.cos(phase), -weight * np.sin(phase)], axis=0)
    return np.pad(table, ((0, 0), (0, LANES - table.shape[1]))).astype(jnp.bfloat16)


def owner_columns(owners_ref, rows, source, width):
    block = source // width
    owner = jnp.zeros_like(source)
    for which in range(OWNERS):
        owner = jnp.where(block == which, owners_ref[which], owner)
    return owner * width + lax.rem(source, width)


def pick_rows(columns, mask_ref):
    stations = lax.broadcasted_iota(jnp.int32, columns.shape, 1)
    chosen = jnp.where(stations == columns, 1.0, 0.0).astype(jnp.bfloat16)
    mask = mask_ref[...].astype(jnp.float32).astype(jnp.bfloat16)
    return lax.dot_general(
        chosen, mask, (((1,), (1,)), ((), ())), preferred_element_type=jnp.float32
    )


def whiten(rows, forward_ref, masks):
    half_len = forward_ref.shape[1] // 2
    spectrum = jnp.dot(rows, forward_ref[...], preferred_element_type=jnp.float32)
    real_part = spectrum[:, :half_len]
    imag_part = spectrum[:, half_len:]
    magnitude = jnp.sqrt(real_part * real_part + imag_part * imag_part)
    level = jnp.mean(magnitude, axis=-1, keepdims=True)
    factor = masks / (magnitude + 0.3 * level + 1e-06)
    return (
        (real_part * factor).astype(jnp.bfloat16).astype(jnp.float32),
        (imag_part * factor).astype(jnp.bfloat16).astype(jnp.float32),
    )


def cross_kernel(
    place_ref, owners_ref, own_ref, src_ref, mask_ref, forward_ref, lag_ref, out_ref, src_re, src_im
):
    first_window, sta_pos = place_ref[0], place_ref[1]
    sources = src_ref.shape[0] // SHARE
    width = own_ref.shape[0] // SHARE
    stations = mask_ref.shape[1]
    both = sources + width
    row = lax.broadcasted_iota(jnp.int32, (both, stations), 0)
    columns = jnp.where(
        row < sources,
        owner_columns(owners_ref, both, row, width),
        sta_pos * width + row - sources,
    )
    alive = pick_rows(columns, mask_ref)
    window = lax.broadcasted_iota(jnp.int32, alive.shape, 1)
    now = [
        jnp.sum(jnp.where(window == first_window + w, alive, 0.0), axis=1, keepdims=True)
        for w in range(SHARE)
    ]
    src_masks = jnp.concatenate([m[:sources] for m in now], axis=0)
    own_masks = jnp.concatenate([m[sources:] for m in now], axis=0)
    own_re, own_im = whiten(own_ref[...], forward_ref, own_masks)
    src_re[...], src_im[...] = whiten(src_ref[...], forward_ref, src_masks)
    half_len = own_re.shape[1]
    crossed = []
    for source in range(sources):
        real_sum = jnp.zeros((width, half_len), jnp.float32)
        imag_sum = jnp.zeros((width, half_len), jnp.float32)
        for w in range(SHARE):
            at = w * sources + source
            re, im = src_re[at : at + 1, :], src_im[at : at + 1, :]
            mine_re = own_re[w * width : (w + 1) * width]
            mine_im = own_im[w * width : (w + 1) * width]
            real_sum = real_sum + (mine_re * re + mine_im * im)
            imag_sum = imag_sum + (mine_im * re - mine_re * im)
        crossed.append(jnp.concatenate([real_sum, imag_sum], axis=1))
    for first in range(0, sources, 16):
        block = jnp.concatenate(crossed[first : first + 16], axis=0).astype(jnp.bfloat16)
        out_ref[first * width : (first + 16) * width, :] = jnp.dot(
            block, lag_ref[...], preferred_element_type=jnp.float32
        ).astype(out_ref.dtype)


def final_kernel(place_ref, owners_ref, parts_ref, mask_ref, out_ref):
    first_source, sta_pos = place_ref[0], place_ref[1]
    width, src_dev, lags = out_ref.shape
    rows = width * src_dev
    stations = mask_ref.shape[1]
    row = lax.broadcasted_iota(jnp.int32, (2 * rows, stations), 0)
    source = first_source + lax.rem(row, rows) // width
    columns = jnp.where(
        row < rows,
        sta_pos * width + lax.rem(row, width),
        owner_columns(owners_ref, 2 * rows, source, width),
    )
    alive = pick_rows(columns, mask_ref)
    counts = jnp.sum(alive[:rows] * alive[rows:], axis=1, keepdims=True)
    total = parts_ref[0:rows, :].astype(jnp.float32)
    for part in range(1, parts_ref.shape[0] // rows):
        total = total + parts_ref[part * rows : (part + 1) * rows, :].astype(jnp.float32)
    total = total / jnp.sqrt(jnp.maximum(counts, 1.0))
    for which in range(src_dev):
        out_ref[:, which, :] = total[which * width : (which + 1) * width, :lags]


def in_vmem():
    return pl.BlockSpec(memory_space=pltpu.VMEM)


def in_smem():
    return pl.BlockSpec(memory_space=pltpu.SMEM)


def on_device(record, alive_mask, owners):
    w_dev, sta_dev, samples = record.shape
    half_len = samples // 2
    sources = OWNERS * sta_dev
    forward = jnp.asarray(forward_table(samples, half_len))
    lag_rows = jnp.asarray(lag_table(samples, half_len, MAXLAG))
    day_count, sta_count = lax.axis_size("day"), lax.axis_size("sta")
    day_pos, sta_pos = lax.axis_index("day"), lax.axis_index("sta")
    src_dev = sources // day_count

    spread = jnp.broadcast_to(
        record.reshape(1, 2, 1, 2, sta_dev, samples),
        (sta_count // 8, 2, 2, 2, sta_dev, samples),
    ).reshape(sta_count, sta_dev, samples)
    everyone = lax.all_to_all(spread, "sta", 0, 0)
    chosen = jnp.concatenate(
        [lax.dynamic_slice_in_dim(everyone, owners[which], 1, 0) for which in range(OWNERS)], axis=0
    )
    quads = [
        [8 * pair + 4 * odd + 2 * far + core for odd in range(2) for core in range(2)]
        for pair in range(sta_count // 8)
        for far in range(2)
    ]
    gathered = lax.all_gather(chosen, "sta", axis_index_groups=quads)

    pieces = pl.pallas_call(
        cross_kernel,
        out_shape=jax.ShapeDtypeStruct((sources * sta_dev, LANES), jnp.bfloat16),
        in_specs=[in_smem(), in_smem()] + [in_vmem()] * 5,
        out_specs=in_vmem(),
        scratch_shapes=[pltpu.VMEM((w_dev * sources, half_len), jnp.float32)] * 2,
        compiler_params=pltpu.CompilerParams(vmem_limit_bytes=24 * 2**20),
        name="cross_lags",
    )(
        jnp.stack([day_pos * w_dev, sta_pos]).astype(jnp.int32),
        owners,
        record.reshape(w_dev * sta_dev, samples),
        gathered.reshape(w_dev * sources, samples),
        alive_mask,
        forward,
        lag_rows,
    )
    rows = src_dev * sta_dev
    parts = lax.all_to_all(pieces.reshape(day_count, rows, LANES), "day", 0, 0)
    return pl.pallas_call(
        final_kernel,
        out_shape=jax.ShapeDtypeStruct((sta_dev, src_dev, 2 * MAXLAG + 1), jnp.float32),
        in_specs=[in_smem(), in_smem()] + [in_vmem()] * 2,
        out_specs=in_vmem(),
        compiler_params=pltpu.CompilerParams(vmem_limit_bytes=16 * 2**20),
        name="sum_parts",
    )(
        jnp.stack([day_pos * src_dev, sta_pos]).astype(jnp.int32),
        owners,
        parts.reshape(day_count * rows, LANES),
        alive_mask,
    )


def solution(mesh):
    return jax.shard_map(
        on_device,
        mesh=mesh,
        in_specs=(P("day", "sta", None), P(), P()),
        out_specs=P("sta", "day", None),
        check_vma=False,
    )
```

```python
import math

import jax
import jax.numpy as jnp
import numpy as np
from jax import lax
from jax.experimental import pallas as pl
from jax.experimental.pallas import tpu as pltpu
from jax.sharding import PartitionSpec as P

MAXLAG = 128
OWNERS = 4
LANES = 384
SHARE = 4


def forward_table(samples, half_len):
    times = np.arange(samples)[:, None]
    bins = np.arange(1, half_len + 1)[None, :]
    phase = (times * bins % samples).astype(np.float32) * np.float32(2.0 * math.pi / samples)
    return np.concatenate([np.cos(phase), -np.sin(phase)], axis=1).astype(jnp.bfloat16)


def lag_table(samples, half_len, reach):
    bins = np.arange(1, half_len + 1)[:, None]
    shifts = np.arange(-reach, reach + 1)[None, :]
    phase = (bins * shifts % samples).astype(np.float32) * np.float32(2.0 * math.pi / samples)
    weight = (np.where(bins == half_len, 1.0, 2.0) / math.sqrt(samples)).astype(np.float32)
    table = np.concatenate([weight * np.cos(phase), -weight * np.sin(phase)], axis=0)
    return np.pad(table, ((0, 0), (0, LANES - table.shape[1]))).astype(jnp.bfloat16)


def owner_columns(owners_ref, source, width):
    block = source // width
    owner = jnp.zeros_like(source)
    for which in range(OWNERS):
        owner = jnp.where(block == which, owners_ref[which], owner)
    return owner * width + lax.rem(source, width)


def pick_rows(columns, mask_ref):
    stations = lax.broadcasted_iota(jnp.int32, columns.shape, 1)
    chosen = jnp.where(stations == columns, 1.0, 0.0).astype(jnp.bfloat16)
    mask = mask_ref[...].astype(jnp.float32).astype(jnp.bfloat16)
    return lax.dot_general(
        chosen, mask, (((1,), (1,)), ((), ())), preferred_element_type=jnp.float32
    )


def whiten(rows, forward_ref, masks):
    half_len = forward_ref.shape[1] // 2
    spectrum = jnp.dot(rows, forward_ref[...], preferred_element_type=jnp.float32)
    real_part = spectrum[:, :half_len]
    imag_part = spectrum[:, half_len:]
    magnitude = jnp.sqrt(real_part * real_part + imag_part * imag_part)
    level = jnp.mean(magnitude, axis=-1, keepdims=True)
    factor = masks / (magnitude + 0.3 * level + 1e-06)
    return (
        (real_part * factor).astype(jnp.bfloat16).astype(jnp.float32),
        (imag_part * factor).astype(jnp.bfloat16).astype(jnp.float32),
    )


def prepare_kernel(
    place_ref, owners_ref, own_ref, mask_ref, forward_ref, white_ref, masks_ref, scale_ref
):
    day_pos, sta_pos = place_ref[0], place_ref[1]
    sources = masks_ref.shape[0] // SHARE
    width = own_ref.shape[0] // SHARE
    stations = mask_ref.shape[1]
    rows = scale_ref.shape[0]
    src_dev = rows // width
    first_window = day_pos * SHARE
    row = lax.broadcasted_iota(jnp.int32, (sources + 2 * rows, stations), 0)
    last = row - sources - rows
    columns = jnp.where(
        row < sources,
        owner_columns(owners_ref, row, width),
        jnp.where(
            last < 0,
            sta_pos * width + lax.rem(row - sources, width),
            owner_columns(owners_ref, day_pos * src_dev + last // width, width),
        ),
    )
    alive = pick_rows(columns, mask_ref)
    window = lax.broadcasted_iota(jnp.int32, alive.shape, 1)
    now = [
        jnp.sum(jnp.where(window == first_window + w, alive, 0.0), axis=1, keepdims=True)
        for w in range(SHARE)
    ]
    for w in range(SHARE):
        masks_ref[w * sources : (w + 1) * sources, :] = jnp.broadcast_to(
            now[w][:sources], (sources, masks_ref.shape[1])
        )
    own_masks = jnp.concatenate([m[sources : sources + width] for m in now], axis=0)
    real_part, imag_part = whiten(own_ref[...], forward_ref, own_masks)
    white_ref[...] = jnp.concatenate([real_part, imag_part], axis=1)
    counts = jnp.sum(
        alive[sources : sources + rows] * alive[sources + rows :], axis=1, keepdims=True
    )
    scale_ref[...] = jnp.broadcast_to(1.0 / jnp.sqrt(jnp.maximum(counts, 1.0)), scale_ref.shape)


def cross_kernel(
    white_ref, tiles_ref, masks_ref, forward_ref, lag_hbm, out_ref, src_re, src_im, lag_ref, sem
):
    fetch = pltpu.make_async_copy(lag_hbm, lag_ref, sem)
    fetch.start()
    sources = masks_ref.shape[0] // SHARE
    width = white_ref.shape[0] // SHARE
    half_len = src_re.shape[1]
    tiles = tiles_ref.shape[0] // sources
    wide = tiles // SHARE
    rows = []
    for w in range(SHARE):
        at = [(t % 2) * (tiles // 2) + t // 2 for t in range(w * wide, (w + 1) * wide)]
        rows.append(
            jnp.concatenate([tiles_ref[a * sources : (a + 1) * sources, :] for a in at], axis=1)
        )
    src_re[...], src_im[...] = whiten(
        jnp.concatenate(rows, axis=0), forward_ref, masks_ref[:, 0:1]
    )
    crossed = []
    for source in range(sources):
        real_sum = jnp.zeros((width, half_len), jnp.float32)
        imag_sum = jnp.zeros((width, half_len), jnp.float32)
        for w in range(SHARE):
            at = w * sources + source
            re, im = src_re[at : at + 1, :], src_im[at : at + 1, :]
            mine_re = white_ref[w * width : (w + 1) * width, :half_len]
            mine_im = white_ref[w * width : (w + 1) * width, half_len:]
            real_sum = real_sum + (mine_re * re + mine_im * im)
            imag_sum = imag_sum + (mine_im * re - mine_re * im)
        crossed.append(jnp.concatenate([real_sum, imag_sum], axis=1))
    fetch.wait()
    for first in range(0, sources, 16):
        block = jnp.concatenate(crossed[first : first + 16], axis=0).astype(jnp.bfloat16)
        out_ref[first * width : (first + 16) * width, :] = jnp.dot(
            block, lag_ref[...], preferred_element_type=jnp.float32
        ).astype(out_ref.dtype)


def final_kernel(parts_ref, scale_ref, out_ref):
    width, src_dev, lags = out_ref.shape
    rows = width * src_dev
    total = parts_ref[0:rows, :].astype(jnp.float32)
    for part in range(1, parts_ref.shape[0] // rows):
        total = total + parts_ref[part * rows : (part + 1) * rows, :].astype(jnp.float32)
    total = total * scale_ref[:, 0:1]
    for which in range(src_dev):
        out_ref[:, which, :] = total[which * width : (which + 1) * width, :lags]


def in_vmem():
    return pl.BlockSpec(memory_space=pltpu.VMEM)


def in_smem():
    return pl.BlockSpec(memory_space=pltpu.SMEM)


def on_device(record, alive_mask, owners):
    w_dev, sta_dev, samples = record.shape
    half_len = samples // 2
    sources = OWNERS * sta_dev
    forward = jnp.asarray(forward_table(samples, half_len))
    lag_rows = jnp.asarray(lag_table(samples, half_len, MAXLAG))
    day_count, sta_count = lax.axis_size("day"), lax.axis_size("sta")
    day_pos, sta_pos = lax.axis_index("day"), lax.axis_index("sta")
    src_dev = sources // day_count
    rows = src_dev * sta_dev
    place = jnp.stack([day_pos, sta_pos]).astype(jnp.int32)

    tiles = record.reshape(w_dev, sta_dev, sta_count // w_dev, -1)
    tiles = tiles.transpose(0, 2, 1, 3).reshape(sta_count, sta_dev, -1)
    everyone = lax.all_to_all(tiles, "sta", 0, 0)

    white, masks, scale = pl.pallas_call(
        prepare_kernel,
        out_shape=[
            jax.ShapeDtypeStruct((w_dev * sta_dev, samples), jnp.float32),
            jax.ShapeDtypeStruct((w_dev * sources, 128), jnp.float32),
            jax.ShapeDtypeStruct((rows, 128), jnp.float32),
        ],
        in_specs=[in_smem(), in_smem()] + [in_vmem()] * 3,
        out_specs=[in_vmem()] * 3,
        compiler_params=pltpu.CompilerParams(vmem_limit_bytes=16 * 2**20),
        cost_estimate=pl.CostEstimate(
            flops=2 * w_dev * sta_dev * samples * samples,
            bytes_accessed=2 * samples * samples,
            transcendentals=w_dev * sta_dev * samples,
        ),
        name="prepare",
    )(place, owners, record.reshape(w_dev * sta_dev, samples), alive_mask, forward)

    chosen = jnp.concatenate(
        [lax.dynamic_slice_in_dim(everyone, owners[which], 1, 0) for which in range(OWNERS)], axis=0
    )
    cores = [[2 * chip + core for chip in range(sta_count // 2)] for core in range(2)]
    pairs = [[2 * chip, 2 * chip + 1] for chip in range(sta_count // 2)]
    half = lax.all_to_all(
        jnp.broadcast_to(chosen[None], (sta_count // 2,) + chosen.shape),
        "sta", 0, 0, axis_index_groups=cores,
    )
    gathered = lax.all_gather(half, "sta", axis_index_groups=pairs)

    pieces = pl.pallas_call(
        cross_kernel,
        out_shape=jax.ShapeDtypeStruct((sources * sta_dev, LANES), jnp.bfloat16),
        in_specs=[in_vmem()] * 4 + [pl.BlockSpec(memory_space=pl.ANY)],
        out_specs=in_vmem(),
        scratch_shapes=[pltpu.VMEM((w_dev * sources, half_len), jnp.float32)] * 2
        + [pltpu.VMEM((samples, LANES), jnp.bfloat16), pltpu.SemaphoreType.DMA],
        compiler_params=pltpu.CompilerParams(vmem_limit_bytes=24 * 2**20),
        name="cross_lags",
    )(white, gathered.reshape(sta_count * sources, -1), masks, forward, lag_rows)
    parts = lax.all_to_all(pieces.reshape(day_count, rows, LANES), "day", 0, 0)
    return pl.pallas_call(
        final_kernel,
        out_shape=jax.ShapeDtypeStruct((sta_dev, src_dev, 2 * MAXLAG + 1), jnp.float32),
        in_specs=[in_vmem()] * 2,
        out_specs=in_vmem(),
        compiler_params=pltpu.CompilerParams(vmem_limit_bytes=16 * 2**20),
        name="sum_parts",
    )(parts.reshape(day_count * rows, LANES), scale)


def solution(mesh):
    return jax.shard_map(
        on_device,
        mesh=mesh,
        in_specs=(P("day", "sta", None), P(), P()),
        out_specs=P("sta", "day", None),
        check_vma=False,
    )
```

```python
import math

import jax
import jax.numpy as jnp
import numpy as np
from jax import lax
from jax.experimental import pallas as pl
from jax.experimental.pallas import tpu as pltpu
from jax.sharding import PartitionSpec as P

MAXLAG = 128
OWNERS = 4
LANES = 384
SHARE = 4


def forward_table(samples, half_len):
    times = np.arange(samples)[:, None]
    bins = np.arange(1, half_len + 1)[None, :]
    phase = (times * bins % samples).astype(np.float32) * np.float32(2.0 * math.pi / samples)
    return np.concatenate([np.cos(phase), -np.sin(phase)], axis=1).astype(jnp.bfloat16)


def lag_table(samples, half_len, reach):
    bins = np.arange(1, half_len + 1)[:, None]
    shifts = np.arange(-reach, reach + 1)[None, :]
    phase = (bins * shifts % samples).astype(np.float32) * np.float32(2.0 * math.pi / samples)
    weight = (np.where(bins == half_len, 1.0, 2.0) / math.sqrt(samples)).astype(np.float32)
    table = np.concatenate([weight * np.cos(phase), -weight * np.sin(phase)], axis=0)
    return np.pad(table, ((0, 0), (0, LANES - table.shape[1]))).astype(jnp.bfloat16)


def owner_columns(owners_ref, source, width):
    block = source // width
    owner = jnp.zeros_like(source)
    for which in range(OWNERS):
        owner = jnp.where(block == which, owners_ref[which], owner)
    return owner * width + lax.rem(source, width)


def pick_rows(columns, mask_ref):
    stations = lax.broadcasted_iota(jnp.int32, columns.shape, 1)
    chosen = jnp.where(stations == columns, 1.0, 0.0).astype(jnp.bfloat16)
    mask = mask_ref[...].astype(jnp.float32).astype(jnp.bfloat16)
    return lax.dot_general(
        chosen, mask, (((1,), (1,)), ((), ())), preferred_element_type=jnp.float32
    )


def whiten(rows, forward_ref, masks):
    half_len = forward_ref.shape[1] // 2
    spectrum = jnp.dot(rows, forward_ref[...], preferred_element_type=jnp.float32)
    real_part = spectrum[:, :half_len]
    imag_part = spectrum[:, half_len:]
    magnitude = jnp.sqrt(real_part * real_part + imag_part * imag_part)
    level = jnp.mean(magnitude, axis=-1, keepdims=True)
    factor = masks / (magnitude + 0.3 * level + 1e-06)
    return (
        (real_part * factor).astype(jnp.bfloat16).astype(jnp.float32),
        (imag_part * factor).astype(jnp.bfloat16).astype(jnp.float32),
    )


def prepare_kernel(
    place_ref, owners_ref, own_ref, mask_ref, forward_ref, white_ref, masks_ref, scale_ref
):
    day_pos, sta_pos = place_ref[0], place_ref[1]
    sources = masks_ref.shape[0] // SHARE
    width = own_ref.shape[0] // SHARE
    stations = mask_ref.shape[1]
    rows = scale_ref.shape[0]
    src_dev = rows // width
    first_window = day_pos * SHARE
    row = lax.broadcasted_iota(jnp.int32, (sources + 2 * rows, stations), 0)
    last = row - sources - rows
    columns = jnp.where(
        row < sources,
        owner_columns(owners_ref, row, width),
        jnp.where(
            last < 0,
            sta_pos * width + lax.rem(row - sources, width),
            owner_columns(owners_ref, day_pos * src_dev + last // width, width),
        ),
    )
    alive = pick_rows(columns, mask_ref)
    window = lax.broadcasted_iota(jnp.int32, alive.shape, 1)
    now = [
        jnp.sum(jnp.where(window == first_window + w, alive, 0.0), axis=1, keepdims=True)
        for w in range(SHARE)
    ]
    for w in range(SHARE):
        masks_ref[w * sources : (w + 1) * sources, :] = jnp.broadcast_to(
            now[w][:sources], (sources, masks_ref.shape[1])
        )
    own_masks = jnp.concatenate([m[sources : sources + width] for m in now], axis=0)
    real_part, imag_part = whiten(own_ref[...], forward_ref, own_masks)
    white_ref[...] = jnp.concatenate([real_part, imag_part], axis=1)
    counts = jnp.sum(
        alive[sources : sources + rows] * alive[sources + rows :], axis=1, keepdims=True
    )
    scale_ref[...] = jnp.broadcast_to(1.0 / jnp.sqrt(jnp.maximum(counts, 1.0)), scale_ref.shape)


def pick_kernel(owners_ref, tiles_ref, out_ref):
    picked = jnp.concatenate([tiles_ref[owners_ref[which]] for which in range(OWNERS)], axis=0)
    for copy in range(out_ref.shape[0]):
        out_ref[copy] = picked


def cross_kernel(
    white_ref, tiles_ref, masks_ref, forward_ref, lag_hbm, out_ref, src_re, src_im, lag_ref, sem
):
    fetch = pltpu.make_async_copy(lag_hbm, lag_ref, sem)
    fetch.start()
    sources = masks_ref.shape[0] // SHARE
    width = white_ref.shape[0] // SHARE
    half_len = src_re.shape[1]
    tiles = tiles_ref.shape[0] // sources
    wide = tiles // SHARE
    rows = []
    for w in range(SHARE):
        at = [(t % 2) * (tiles // 2) + t // 2 for t in range(w * wide, (w + 1) * wide)]
        rows.append(
            jnp.concatenate([tiles_ref[a * sources : (a + 1) * sources, :] for a in at], axis=1)
        )
    src_re[...], src_im[...] = whiten(
        jnp.concatenate(rows, axis=0), forward_ref, masks_ref[:, 0:1]
    )
    crossed = []
    for source in range(sources):
        real_sum = jnp.zeros((width, half_len), jnp.float32)
        imag_sum = jnp.zeros((width, half_len), jnp.float32)
        for w in range(SHARE):
            at = w * sources + source
            re, im = src_re[at : at + 1, :], src_im[at : at + 1, :]
            mine_re = white_ref[w * width : (w + 1) * width, :half_len]
            mine_im = white_ref[w * width : (w + 1) * width, half_len:]
            real_sum = real_sum + (mine_re * re + mine_im * im)
            imag_sum = imag_sum + (mine_im * re - mine_re * im)
        crossed.append(jnp.concatenate([real_sum, imag_sum], axis=1))
    fetch.wait()
    for first in range(0, sources, 16):
        block = jnp.concatenate(crossed[first : first + 16], axis=0).astype(jnp.bfloat16)
        out_ref[first * width : (first + 16) * width, :] = jnp.dot(
            block, lag_ref[...], preferred_element_type=jnp.float32
        ).astype(out_ref.dtype)


def final_kernel(parts_ref, scale_ref, out_ref):
    width, src_dev, lags = out_ref.shape
    rows = width * src_dev
    total = parts_ref[0:rows, :].astype(jnp.float32)
    for part in range(1, parts_ref.shape[0] // rows):
        total = total + parts_ref[part * rows : (part + 1) * rows, :].astype(jnp.float32)
    total = total * scale_ref[:, 0:1]
    for which in range(src_dev):
        out_ref[:, which, :] = total[which * width : (which + 1) * width, :lags]


def in_vmem():
    return pl.BlockSpec(memory_space=pltpu.VMEM)


def in_smem():
    return pl.BlockSpec(memory_space=pltpu.SMEM)


def on_device(record, alive_mask, owners):
    w_dev, sta_dev, samples = record.shape
    half_len = samples // 2
    sources = OWNERS * sta_dev
    forward = jnp.asarray(forward_table(samples, half_len))
    lag_rows = jnp.asarray(lag_table(samples, half_len, MAXLAG))
    day_count, sta_count = lax.axis_size("day"), lax.axis_size("sta")
    day_pos, sta_pos = lax.axis_index("day"), lax.axis_index("sta")
    src_dev = sources // day_count
    rows = src_dev * sta_dev
    place = jnp.stack([day_pos, sta_pos]).astype(jnp.int32)

    tiles = record.reshape(w_dev, sta_dev, sta_count // w_dev, -1)
    tiles = tiles.transpose(0, 2, 1, 3).reshape(sta_count, sta_dev, -1)
    everyone = lax.all_to_all(tiles, "sta", 0, 0)

    white, masks, scale = pl.pallas_call(
        prepare_kernel,
        out_shape=[
            jax.ShapeDtypeStruct((w_dev * sta_dev, samples), jnp.float32),
            jax.ShapeDtypeStruct((w_dev * sources, 128), jnp.float32),
            jax.ShapeDtypeStruct((rows, 128), jnp.float32),
        ],
        in_specs=[in_smem(), in_smem()] + [in_vmem()] * 3,
        out_specs=[in_vmem()] * 3,
        compiler_params=pltpu.CompilerParams(vmem_limit_bytes=16 * 2**20),
        cost_estimate=pl.CostEstimate(
            flops=2 * w_dev * sta_dev * samples * samples,
            bytes_accessed=2 * samples * samples,
            transcendentals=w_dev * sta_dev * samples,
        ),
        name="prepare",
    )(place, owners, record.reshape(w_dev * sta_dev, samples), alive_mask, forward)

    everyone, white, masks, scale = lax.optimization_barrier((everyone, white, masks, scale))
    copies = pl.pallas_call(
        pick_kernel,
        out_shape=jax.ShapeDtypeStruct((sta_count // 2, sources, tiles.shape[2]), record.dtype),
        in_specs=[in_smem(), in_vmem()],
        out_specs=in_vmem(),
        compiler_params=pltpu.CompilerParams(vmem_limit_bytes=8 * 2**20),
        name="pick_owners",
    )(owners, everyone)
    cores = [[2 * chip + core for chip in range(sta_count // 2)] for core in range(2)]
    pairs = [[2 * chip, 2 * chip + 1] for chip in range(sta_count // 2)]
    half = lax.all_to_all(copies, "sta", 0, 0, axis_index_groups=cores)
    gathered = lax.all_gather(half, "sta", axis_index_groups=pairs)

    pieces = pl.pallas_call(
        cross_kernel,
        out_shape=jax.ShapeDtypeStruct((sources * sta_dev, LANES), jnp.bfloat16),
        in_specs=[in_vmem()] * 4 + [pl.BlockSpec(memory_space=pltpu.HBM)],
        out_specs=in_vmem(),
        scratch_shapes=[pltpu.VMEM((w_dev * sources, half_len), jnp.float32)] * 2
        + [pltpu.VMEM((samples, LANES), jnp.bfloat16), pltpu.SemaphoreType.DMA],
        compiler_params=pltpu.CompilerParams(vmem_limit_bytes=24 * 2**20),
        name="cross_lags",
    )(white, gathered.reshape(sta_count * sources, -1), masks, forward, lag_rows)
    parts = lax.all_to_all(pieces.reshape(day_count, rows, LANES), "day", 0, 0)
    return pl.pallas_call(
        final_kernel,
        out_shape=jax.ShapeDtypeStruct((sta_dev, src_dev, 2 * MAXLAG + 1), jnp.float32),
        in_specs=[in_vmem()] * 2,
        out_specs=in_vmem(),
        compiler_params=pltpu.CompilerParams(vmem_limit_bytes=16 * 2**20),
        name="sum_parts",
    )(parts.reshape(day_count * rows, LANES), scale)


def solution(mesh):
    return jax.shard_map(
        on_device,
        mesh=mesh,
        in_specs=(P("day", "sta", None), P(), P()),
        out_specs=P("sta", "day", None),
        check_vma=False,
    )
```

```python
import math

import jax
import jax.numpy as jnp
import numpy as np
from jax import lax
from jax.experimental import pallas as pl
from jax.experimental.pallas import tpu as pltpu
from jax.sharding import PartitionSpec as P

MAXLAG = 128
OWNERS = 4
LANES = 384
SHARE = 4
SOURCES = 32


def forward_table(samples, half_len):
    times = np.arange(samples)[:, None]
    bins = np.arange(1, half_len + 1)[None, :]
    phase = (times * bins % samples).astype(np.float32) * np.float32(2.0 * math.pi / samples)
    return np.concatenate([np.cos(phase), -np.sin(phase)], axis=1).astype(jnp.bfloat16)


def lag_table(samples, half_len, reach):
    bins = np.arange(1, half_len + 1)[:, None]
    shifts = np.arange(-reach, reach + 1)[None, :]
    phase = (bins * shifts % samples).astype(np.float32) * np.float32(2.0 * math.pi / samples)
    weight = (np.where(bins == half_len, 1.0, 2.0) / math.sqrt(samples)).astype(np.float32)
    table = np.concatenate([weight * np.cos(phase), -weight * np.sin(phase)], axis=0)
    return np.pad(table, ((0, 0), (0, LANES - table.shape[1]))).astype(jnp.bfloat16)


def owner_columns(owners_ref, source, width):
    block = source // width
    owner = jnp.zeros_like(source)
    for which in range(OWNERS):
        owner = jnp.where(block == which, owners_ref[which], owner)
    return owner * width + lax.rem(source, width)


def pick_rows(columns, mask_ref):
    stations = lax.broadcasted_iota(jnp.int32, columns.shape, 1)
    chosen = jnp.where(stations == columns, 1.0, 0.0).astype(jnp.bfloat16)
    mask = mask_ref[...].astype(jnp.float32).astype(jnp.bfloat16)
    return lax.dot_general(
        chosen, mask, (((1,), (1,)), ((), ())), preferred_element_type=jnp.float32
    )


def whiten(rows, forward_ref, masks):
    half_len = forward_ref.shape[1] // 2
    spectrum = jnp.dot(rows, forward_ref[...], preferred_element_type=jnp.float32)
    real_part = spectrum[:, :half_len]
    imag_part = spectrum[:, half_len:]
    magnitude = jnp.sqrt(real_part * real_part + imag_part * imag_part)
    level = jnp.mean(magnitude, axis=-1, keepdims=True)
    factor = masks / (magnitude + 0.3 * level + 1e-06)
    return (
        (real_part * factor).astype(jnp.bfloat16).astype(jnp.float32),
        (imag_part * factor).astype(jnp.bfloat16).astype(jnp.float32),
    )


def mask_kernel(place_ref, owners_ref, mask_ref, masks_ref, scale_ref):
    day_pos, sta_pos = place_ref[0], place_ref[1]
    stations = mask_ref.shape[1]
    rows = scale_ref.shape[0]
    sources = SOURCES
    width = sources // OWNERS
    src_dev = rows // width
    first_window = day_pos * SHARE
    row = lax.broadcasted_iota(jnp.int32, (sources + 2 * rows, stations), 0)
    last = row - sources - rows
    columns = jnp.where(
        row < sources,
        owner_columns(owners_ref, row, width),
        jnp.where(
            last < 0,
            sta_pos * width + lax.rem(row - sources, width),
            owner_columns(owners_ref, day_pos * src_dev + last // width, width),
        ),
    )
    alive = pick_rows(columns, mask_ref)
    window = lax.broadcasted_iota(jnp.int32, alive.shape, 1)
    now = [
        jnp.sum(jnp.where(window == first_window + w, alive, 0.0), axis=1, keepdims=True)
        for w in range(SHARE)
    ]
    column = jnp.concatenate(
        [m[:sources] for m in now] + [m[sources : sources + width] for m in now], axis=0
    )
    masks_ref[...] = jnp.broadcast_to(column, masks_ref.shape)
    counts = jnp.sum(
        alive[sources : sources + rows] * alive[sources + rows :], axis=1, keepdims=True
    )
    scale_ref[...] = jnp.broadcast_to(1.0 / jnp.sqrt(jnp.maximum(counts, 1.0)), scale_ref.shape)


def pick_kernel(owners_ref, tiles_ref, out_ref):
    picked = jnp.concatenate([tiles_ref[owners_ref[which]] for which in range(OWNERS)], axis=0)
    for copy in range(out_ref.shape[0]):
        out_ref[copy] = picked


def cross_kernel(
    own_ref, tiles_ref, masks_ref, forward_ref, lag_ref, out_ref, white_re, white_im
):
    width = own_ref.shape[0] // SHARE
    sources = masks_ref.shape[0] // SHARE - width
    half_len = white_re.shape[1]
    tiles = tiles_ref.shape[0] // sources
    wide = tiles // SHARE
    rows = []
    for w in range(SHARE):
        rows.append(
            jnp.concatenate(
                [
                    tiles_ref[t * sources : (t + 1) * sources, :]
                    for t in range(w * wide, (w + 1) * wide)
                ],
                axis=1,
            )
        )
    rows.append(own_ref[...])
    white_re[...], white_im[...] = whiten(
        jnp.concatenate(rows, axis=0), forward_ref, masks_ref[:, 0:1]
    )
    first_own = SHARE * sources
    crossed = []
    for source in range(sources):
        real_sum = jnp.zeros((width, half_len), jnp.float32)
        imag_sum = jnp.zeros((width, half_len), jnp.float32)
        for w in range(SHARE):
            at = w * sources + source
            re, im = white_re[at : at + 1, :], white_im[at : at + 1, :]
            mine = slice(first_own + w * width, first_own + (w + 1) * width)
            mine_re, mine_im = white_re[mine, :], white_im[mine, :]
            real_sum = real_sum + (mine_re * re + mine_im * im)
            imag_sum = imag_sum + (mine_im * re - mine_re * im)
        crossed.append(jnp.concatenate([real_sum, imag_sum], axis=1))
    for first in range(0, sources, 16):
        block = jnp.concatenate(crossed[first : first + 16], axis=0).astype(jnp.bfloat16)
        out_ref[first * width : (first + 16) * width, :] = jnp.dot(
            block, lag_ref[...], preferred_element_type=jnp.float32
        ).astype(out_ref.dtype)


def final_kernel(parts_ref, scale_ref, out_ref):
    width, src_dev, lags = out_ref.shape
    rows = width * src_dev
    total = parts_ref[0:rows, :].astype(jnp.float32)
    for part in range(1, parts_ref.shape[0] // rows):
        total = total + parts_ref[part * rows : (part + 1) * rows, :].astype(jnp.float32)
    total = total * scale_ref[:, 0:1]
    for which in range(src_dev):
        out_ref[:, which, :] = total[which * width : (which + 1) * width, :lags]


def in_vmem():
    return pl.BlockSpec(memory_space=pltpu.VMEM)


def in_smem():
    return pl.BlockSpec(memory_space=pltpu.SMEM)


def on_device(record, alive_mask, owners):
    w_dev, sta_dev, samples = record.shape
    half_len = samples // 2
    sources = OWNERS * sta_dev
    forward = jnp.asarray(forward_table(samples, half_len))
    lag_rows = jnp.asarray(lag_table(samples, half_len, MAXLAG))
    day_count, sta_count = lax.axis_size("day"), lax.axis_size("sta")
    day_pos, sta_pos = lax.axis_index("day"), lax.axis_index("sta")
    src_dev = sources // day_count
    rows = src_dev * sta_dev
    place = jnp.stack([day_pos, sta_pos]).astype(jnp.int32)

    tiles = record.reshape(w_dev, sta_dev, sta_count // w_dev, -1)
    tiles = tiles.transpose(0, 2, 1, 3).reshape(sta_count, sta_dev, -1)
    everyone = lax.all_to_all(tiles, "sta", 0, 0)

    masks, scale = pl.pallas_call(
        mask_kernel,
        out_shape=[
            jax.ShapeDtypeStruct((w_dev * (sources + sta_dev), 128), jnp.float32),
            jax.ShapeDtypeStruct((rows, 128), jnp.float32),
        ],
        in_specs=[in_smem(), in_smem(), in_vmem()],
        out_specs=[in_vmem()] * 2,
        compiler_params=pltpu.CompilerParams(vmem_limit_bytes=16 * 2**20),
        cost_estimate=pl.CostEstimate(
            flops=2000000000, bytes_accessed=2097152, transcendentals=0
        ),
        name="masks",
    )(place, owners, alive_mask)
    everyone, masks, scale = lax.optimization_barrier((everyone, masks, scale))
    copies = pl.pallas_call(
        pick_kernel,
        out_shape=jax.ShapeDtypeStruct((sta_count, sources, tiles.shape[2]), record.dtype),
        in_specs=[in_smem(), in_vmem()],
        out_specs=in_vmem(),
        compiler_params=pltpu.CompilerParams(vmem_limit_bytes=8 * 2**20),
        name="pick_owners",
    )(owners, everyone)
    gathered = lax.all_to_all(copies, "sta", 0, 0)

    pieces = pl.pallas_call(
        cross_kernel,
        out_shape=jax.ShapeDtypeStruct((sources * sta_dev, LANES), jnp.bfloat16),
        in_specs=[in_vmem()] * 5,
        out_specs=in_vmem(),
        scratch_shapes=[pltpu.VMEM((w_dev * (sources + sta_dev), half_len), jnp.float32)] * 2,
        compiler_params=pltpu.CompilerParams(vmem_limit_bytes=24 * 2**20),
        name="cross_lags",
    )(
        record.reshape(w_dev * sta_dev, samples),
        gathered.reshape(sta_count * sources, -1),
        masks,
        forward,
        lag_rows,
    )
    parts = lax.all_to_all(pieces.reshape(day_count, rows, LANES), "day", 0, 0)
    return pl.pallas_call(
        final_kernel,
        out_shape=jax.ShapeDtypeStruct((sta_dev, src_dev, 2 * MAXLAG + 1), jnp.float32),
        in_specs=[in_vmem()] * 2,
        out_specs=in_vmem(),
        compiler_params=pltpu.CompilerParams(vmem_limit_bytes=16 * 2**20),
        name="sum_parts",
    )(parts.reshape(day_count * rows, LANES), scale)


def solution(mesh):
    return jax.shard_map(
        on_device,
        mesh=mesh,
        in_specs=(P("day", "sta", None), P(), P()),
        out_specs=P("sta", "day", None),
        check_vma=False,
    )
```

```python
import math

import jax
import jax.numpy as jnp
import numpy as np
from jax import lax
from jax.experimental import pallas as pl
from jax.experimental.pallas import tpu as pltpu
from jax.sharding import PartitionSpec as P

MAXLAG = 128
OWNERS = 4
SHARE = 4
SOURCES = 32


def forward_table(samples, half_len):
    times = np.arange(samples)[:, None]
    bins = np.arange(1, half_len + 1)[None, :]
    phase = (times * bins % samples).astype(np.float32) * np.float32(2.0 * math.pi / samples)
    return np.concatenate([np.cos(phase), -np.sin(phase)], axis=1).astype(jnp.bfloat16)


def lag_table(samples, half_len, reach):
    bins = np.arange(1, half_len + 1)[:, None]
    shifts = np.arange(-reach, reach + 1)[None, :]
    phase = (bins * shifts % samples).astype(np.float32) * np.float32(2.0 * math.pi / samples)
    weight = (np.where(bins == half_len, 1.0, 2.0) / math.sqrt(samples)).astype(np.float32)
    table = np.concatenate([weight * np.cos(phase), -weight * np.sin(phase)], axis=0)
    table = table.astype(jnp.bfloat16)
    return table[:, :-1], np.pad(table[:, -1:].T, ((0, 15), (0, 0)))


def owner_columns(owners_ref, source, width):
    block = source // width
    owner = jnp.zeros_like(source)
    for which in range(OWNERS):
        owner = jnp.where(block == which, owners_ref[which], owner)
    return owner * width + lax.rem(source, width)


def pick_rows(columns, mask_ref):
    stations = lax.broadcasted_iota(jnp.int32, columns.shape, 1)
    chosen = jnp.where(stations == columns, 1.0, 0.0).astype(jnp.bfloat16)
    mask = mask_ref[...].astype(jnp.float32).astype(jnp.bfloat16)
    return lax.dot_general(
        chosen, mask, (((1,), (1,)), ((), ())), preferred_element_type=jnp.float32
    )


def whiten(rows, forward_ref, masks):
    half_len = forward_ref.shape[1] // 2
    spectrum = jnp.dot(rows, forward_ref[...], preferred_element_type=jnp.float32)
    real_part = spectrum[:, :half_len]
    imag_part = spectrum[:, half_len:]
    magnitude = jnp.sqrt(real_part * real_part + imag_part * imag_part)
    level = jnp.mean(magnitude, axis=-1, keepdims=True)
    factor = masks / (magnitude + 0.3 * level + 1e-06)
    return (
        (real_part * factor).astype(jnp.bfloat16).astype(jnp.float32),
        (imag_part * factor).astype(jnp.bfloat16).astype(jnp.float32),
    )


def mask_kernel(place_ref, owners_ref, mask_ref, masks_ref, scale_ref):
    day_pos, sta_pos = place_ref[0], place_ref[1]
    stations = mask_ref.shape[1]
    rows = scale_ref.shape[0] // 2
    sources = SOURCES
    width = sources // OWNERS
    src_dev = rows // width
    first_window = day_pos * SHARE
    row = lax.broadcasted_iota(jnp.int32, (sources + 2 * rows, stations), 0)
    last = row - sources - rows
    columns = jnp.where(
        row < sources,
        owner_columns(owners_ref, row, width),
        jnp.where(
            last < 0,
            sta_pos * width + lax.rem(row - sources, width),
            owner_columns(owners_ref, day_pos * src_dev + last // width, width),
        ),
    )
    alive = pick_rows(columns, mask_ref)
    window = lax.broadcasted_iota(jnp.int32, alive.shape, 1)
    now = [
        jnp.sum(jnp.where(window == first_window + w, alive, 0.0), axis=1, keepdims=True)
        for w in range(SHARE)
    ]
    column = jnp.concatenate(
        [m[:sources] for m in now] + [m[sources : sources + width] for m in now], axis=0
    )
    masks_ref[...] = jnp.broadcast_to(column, masks_ref.shape)
    counts = jnp.sum(
        alive[sources : sources + rows] * alive[sources + rows :], axis=1, keepdims=True
    )
    lanes = scale_ref.shape[1]
    scale = jnp.broadcast_to(1.0 / jnp.sqrt(jnp.maximum(counts, 1.0)), (rows, lanes))
    lane = lax.broadcasted_iota(jnp.int32, scale.shape, 1)
    arrives = lax.rem(day_pos * rows, lanes) + lax.broadcasted_iota(jnp.int32, scale.shape, 0)
    scale_ref[...] = jnp.concatenate([scale, jnp.where(lane == arrives, scale, 0.0)], axis=0)


def pick_kernel(owners_ref, tiles_ref, out_ref):
    picked = jnp.concatenate([tiles_ref[owners_ref[which]] for which in range(OWNERS)], axis=0)
    for copy in range(out_ref.shape[0]):
        out_ref[copy] = picked


def cross_kernel(
    own_ref, tiles_ref, masks_ref, forward_ref, lag_ref, last_ref, out_ref, white_re, white_im
):
    width = own_ref.shape[0] // SHARE
    sources = masks_ref.shape[0] // SHARE - width
    half_len = white_re.shape[1]
    tiles = tiles_ref.shape[0] // sources
    wide = tiles // SHARE
    rows = []
    for w in range(SHARE):
        rows.append(
            jnp.concatenate(
                [
                    tiles_ref[t * sources : (t + 1) * sources, :]
                    for t in range(w * wide, (w + 1) * wide)
                ],
                axis=1,
            )
        )
    rows.append(own_ref[...])
    white_re[...], white_im[...] = whiten(
        jnp.concatenate(rows, axis=0), forward_ref, masks_ref[:, 0:1]
    )
    first_own = SHARE * sources
    crossed = []
    for source in range(sources):
        real_sum = jnp.zeros((width, half_len), jnp.float32)
        imag_sum = jnp.zeros((width, half_len), jnp.float32)
        for w in range(SHARE):
            at = w * sources + source
            re, im = white_re[at : at + 1, :], white_im[at : at + 1, :]
            mine = slice(first_own + w * width, first_own + (w + 1) * width)
            mine_re, mine_im = white_re[mine, :], white_im[mine, :]
            real_sum = real_sum + (mine_re * re + mine_im * im)
            imag_sum = imag_sum + (mine_im * re - mine_re * im)
        crossed.append(jnp.concatenate([real_sum, imag_sum], axis=1))
    lanes = out_ref.shape[2]
    piece = sources * width // out_ref.shape[0]
    step = lanes // width
    for first in range(0, sources, step):
        block = jnp.concatenate(crossed[first : first + step], axis=0).astype(jnp.bfloat16)
        lags = jnp.dot(block, lag_ref[...], preferred_element_type=jnp.float32)
        last = lax.dot_general(
            last_ref[...], block, (((1,), (1,)), ((), ())), preferred_element_type=jnp.float32
        )
        for at in range(0, lanes, piece):
            out_ref[(first * width + at) // piece] = jnp.concatenate(
                [lags[at : at + piece, :lanes], lags[at : at + piece, lanes:], last[:8]], axis=0
            ).astype(out_ref.dtype)


def final_kernel(parts_ref, scale_ref, out_ref):
    width, src_dev, lags = out_ref.shape
    rows = width * src_dev
    lanes = parts_ref.shape[2]
    total = parts_ref[0].astype(jnp.float32)
    for part in range(1, parts_ref.shape[0]):
        total = total + parts_ref[part].astype(jnp.float32)
    scale = scale_ref[:rows]
    early = total[:rows] * scale
    late = total[rows : 2 * rows] * scale
    last = jnp.sum(total[2 * rows : 2 * rows + 1] * scale_ref[rows:], axis=1, keepdims=True)
    for which in range(src_dev):
        at = slice(which * width, (which + 1) * width)
        out_ref[:, which, :lanes] = early[at]
        out_ref[:, which, lanes : lags - 1] = late[at]
        out_ref[:, which, lags - 1 :] = last[at]


def in_vmem():
    return pl.BlockSpec(memory_space=pltpu.VMEM)


def in_smem():
    return pl.BlockSpec(memory_space=pltpu.SMEM)


def on_device(record, alive_mask, owners):
    w_dev, sta_dev, samples = record.shape
    half_len = samples // 2
    sources = OWNERS * sta_dev
    forward = jnp.asarray(forward_table(samples, half_len))
    lag_rows, last_row = map(jnp.asarray, lag_table(samples, half_len, MAXLAG))
    day_count, sta_count = lax.axis_size("day"), lax.axis_size("sta")
    day_pos, sta_pos = lax.axis_index("day"), lax.axis_index("sta")
    src_dev = sources // day_count
    rows = src_dev * sta_dev
    place = jnp.stack([day_pos, sta_pos]).astype(jnp.int32)

    tiles = record.reshape(w_dev, sta_dev, sta_count // w_dev, -1)
    tiles = tiles.transpose(0, 2, 1, 3).reshape(sta_count, sta_dev, -1)
    everyone = lax.all_to_all(tiles, "sta", 0, 0)

    masks, scale = pl.pallas_call(
        mask_kernel,
        out_shape=[
            jax.ShapeDtypeStruct((w_dev * (sources + sta_dev), 128), jnp.float32),
            jax.ShapeDtypeStruct((2 * rows, 128), jnp.float32),
        ],
        in_specs=[in_smem(), in_smem(), in_vmem()],
        out_specs=[in_vmem()] * 2,
        compiler_params=pltpu.CompilerParams(vmem_limit_bytes=16 * 2**20),
        cost_estimate=pl.CostEstimate(
            flops=2000000000, bytes_accessed=2097152, transcendentals=0
        ),
        name="masks",
    )(place, owners, alive_mask)
    everyone, masks, scale = lax.optimization_barrier((everyone, masks, scale))
    copies = pl.pallas_call(
        pick_kernel,
        out_shape=jax.ShapeDtypeStruct((sta_count, sources, tiles.shape[2]), record.dtype),
        in_specs=[in_smem(), in_vmem()],
        out_specs=in_vmem(),
        compiler_params=pltpu.CompilerParams(vmem_limit_bytes=8 * 2**20),
        name="pick_owners",
    )(owners, everyone)
    gathered = lax.all_to_all(copies, "sta", 0, 0)

    pieces = pl.pallas_call(
        cross_kernel,
        out_shape=jax.ShapeDtypeStruct((day_count, 2 * rows + 8, 128), jnp.bfloat16),
        in_specs=[in_vmem()] * 6,
        out_specs=in_vmem(),
        scratch_shapes=[pltpu.VMEM((w_dev * (sources + sta_dev), half_len), jnp.float32)] * 2,
        compiler_params=pltpu.CompilerParams(vmem_limit_bytes=24 * 2**20),
        name="cross_lags",
    )(
        record.reshape(w_dev * sta_dev, samples),
        gathered.reshape(sta_count * sources, -1),
        masks,
        forward,
        lag_rows,
        last_row,
    )
    parts = lax.all_to_all(pieces, "day", 0, 0)
    return pl.pallas_call(
        final_kernel,
        out_shape=jax.ShapeDtypeStruct((sta_dev, src_dev, 2 * MAXLAG + 1), jnp.float32),
        in_specs=[in_vmem()] * 2,
        out_specs=in_vmem(),
        compiler_params=pltpu.CompilerParams(vmem_limit_bytes=16 * 2**20),
        name="sum_parts",
    )(parts, scale)


def solution(mesh):
    return jax.shard_map(
        on_device,
        mesh=mesh,
        in_specs=(P("day", "sta", None), P(), P()),
        out_specs=P("sta", "day", None),
        check_vma=False,
    )
```

```python
import math

import jax
import jax.numpy as jnp
import numpy as np
from jax import lax
from jax.experimental import pallas as pl
from jax.experimental.pallas import tpu as pltpu
from jax.sharding import PartitionSpec as P

MAXLAG = 128
OWNERS = 4
SHARE = 4
SOURCES = 32
GROUP = 8


def forward_table(samples, half_len):
    times = np.arange(samples)[:, None]
    bins = np.arange(1, half_len + 1)[None, :]
    phase = (times * bins % samples).astype(np.float32) * np.float32(2.0 * math.pi / samples)
    return np.concatenate([np.cos(phase), -np.sin(phase)], axis=1).astype(jnp.bfloat16)


def lag_table(samples, half_len, reach):
    bins = np.arange(1, half_len + 1)[:, None]
    shifts = np.arange(-reach, reach + 1)[None, :]
    phase = (bins * shifts % samples).astype(np.float32) * np.float32(2.0 * math.pi / samples)
    weight = (np.where(bins == half_len, 1.0, 2.0) / math.sqrt(samples)).astype(np.float32)
    table = np.concatenate([weight * np.cos(phase), -weight * np.sin(phase)], axis=0)
    table = table.astype(jnp.bfloat16)
    return table[:, :-1], np.pad(table[:, -1:].T, ((0, 15), (0, 0)))


def owner_columns(owners_ref, source, width):
    block = source // width
    owner = jnp.zeros_like(source)
    for which in range(OWNERS):
        owner = jnp.where(block == which, owners_ref[which], owner)
    return owner * width + lax.rem(source, width)


def pick_rows(columns, mask_ref):
    stations = lax.broadcasted_iota(jnp.int32, columns.shape, 1)
    chosen = jnp.where(stations == columns, 1.0, 0.0).astype(jnp.bfloat16)
    mask = mask_ref[...].astype(jnp.float32).astype(jnp.bfloat16)
    return lax.dot_general(
        chosen, mask, (((1,), (1,)), ((), ())), preferred_element_type=jnp.float32
    )


def whiten(rows, forward_ref, masks):
    half_len = forward_ref.shape[1] // 2
    spectrum = jnp.dot(rows, forward_ref[...], preferred_element_type=jnp.float32)
    real_part = spectrum[:, :half_len]
    imag_part = spectrum[:, half_len:]
    magnitude = jnp.sqrt(real_part * real_part + imag_part * imag_part)
    level = jnp.mean(magnitude, axis=-1, keepdims=True)
    factor = masks / (magnitude + 0.3 * level + 1e-06)
    return (
        (real_part * factor).astype(jnp.bfloat16).astype(jnp.float32),
        (imag_part * factor).astype(jnp.bfloat16).astype(jnp.float32),
    )


def mask_kernel(place_ref, owners_ref, mask_ref, masks_ref, scale_ref):
    day_pos, sta_pos = place_ref[0], place_ref[1]
    stations = mask_ref.shape[1]
    rows = scale_ref.shape[0] // 2
    sources = SOURCES
    width = sources // OWNERS
    src_dev = rows // width
    first_window = day_pos * SHARE
    row = lax.broadcasted_iota(jnp.int32, (sources + 2 * rows, stations), 0)
    last = row - sources - rows
    columns = jnp.where(
        row < sources,
        owner_columns(owners_ref, row, width),
        jnp.where(
            last < 0,
            sta_pos * width + lax.rem(row - sources, width),
            owner_columns(owners_ref, day_pos * src_dev + last // width, width),
        ),
    )
    alive = pick_rows(columns, mask_ref)
    window = lax.broadcasted_iota(jnp.int32, alive.shape, 1)
    now = [
        jnp.sum(jnp.where(window == first_window + w, alive, 0.0), axis=1, keepdims=True)
        for w in range(SHARE)
    ]
    column = jnp.concatenate(
        [m[:sources] for m in now] + [m[sources : sources + width] for m in now], axis=0
    )
    masks_ref[...] = jnp.broadcast_to(column, masks_ref.shape)
    counts = jnp.sum(
        alive[sources : sources + rows] * alive[sources + rows :], axis=1, keepdims=True
    )
    lanes = scale_ref.shape[1]
    scale = jnp.broadcast_to(1.0 / jnp.sqrt(jnp.maximum(counts, 1.0)), (rows, lanes))
    lane = lax.broadcasted_iota(jnp.int32, scale.shape, 1)
    arrives = lax.rem(day_pos * rows, lanes) + lax.broadcasted_iota(jnp.int32, scale.shape, 0)
    scale_ref[...] = jnp.concatenate([scale, jnp.where(lane == arrives, scale, 0.0)], axis=0)


def pick_kernel(owners_ref, tiles_ref, out_ref):
    picked = jnp.concatenate(
        [
            tiles_ref[owners_ref[which], part]
            for part in range(tiles_ref.shape[1])
            for which in range(OWNERS)
        ],
        axis=0,
    )
    for copy in range(out_ref.shape[0]):
        out_ref[copy] = picked


def cross_kernel(
    own_ref, tiles_ref, masks_ref, forward_ref, lag_ref, last_ref, out_ref, white_re, white_im
):
    width = own_ref.shape[0] // SHARE
    sources = masks_ref.shape[0] // SHARE - width
    half_len = white_re.shape[1]
    tiles = tiles_ref.shape[0] // sources
    wide = tiles // SHARE
    rows = []
    for w in range(SHARE):
        rows.append(
            jnp.concatenate(
                [
                    tiles_ref[t * sources : (t + 1) * sources, :]
                    for t in range(w * wide, (w + 1) * wide)
                ],
                axis=1,
            )
        )
    rows.append(own_ref[...])
    white_re[...], white_im[...] = whiten(
        jnp.concatenate(rows, axis=0), forward_ref, masks_ref[:, 0:1]
    )
    first_own = SHARE * sources
    crossed = []
    for source in range(sources):
        real_sum = jnp.zeros((width, half_len), jnp.float32)
        imag_sum = jnp.zeros((width, half_len), jnp.float32)
        for w in range(SHARE):
            at = w * sources + source
            re, im = white_re[at : at + 1, :], white_im[at : at + 1, :]
            mine = slice(first_own + w * width, first_own + (w + 1) * width)
            mine_re, mine_im = white_re[mine, :], white_im[mine, :]
            real_sum = real_sum + (mine_re * re + mine_im * im)
            imag_sum = imag_sum + (mine_im * re - mine_re * im)
        crossed.append(jnp.concatenate([real_sum, imag_sum], axis=1))
    lanes = out_ref.shape[2]
    piece = sources * width // out_ref.shape[0]
    step = lanes // width
    for first in range(0, sources, step):
        block = jnp.concatenate(crossed[first : first + step], axis=0).astype(jnp.bfloat16)
        lags = jnp.dot(block, lag_ref[...], preferred_element_type=jnp.float32)
        last = lax.dot_general(
            last_ref[...], block, (((1,), (1,)), ((), ())), preferred_element_type=jnp.float32
        )
        for at in range(0, lanes, piece):
            out_ref[(first * width + at) // piece] = jnp.concatenate(
                [lags[at : at + piece, :lanes], lags[at : at + piece, lanes:], last[:8]], axis=0
            ).astype(out_ref.dtype)


def final_kernel(parts_ref, scale_ref, out_ref):
    width, src_dev, lags = out_ref.shape
    rows = width * src_dev
    lanes = parts_ref.shape[2]
    total = parts_ref[0].astype(jnp.float32)
    for part in range(1, parts_ref.shape[0]):
        total = total + parts_ref[part].astype(jnp.float32)
    scale = scale_ref[:rows]
    early = total[:rows] * scale
    late = total[rows : 2 * rows] * scale
    last = jnp.sum(total[2 * rows : 2 * rows + 1] * scale_ref[rows:], axis=1, keepdims=True)
    for which in range(src_dev):
        at = slice(which * width, (which + 1) * width)
        out_ref[:, which, :lanes] = early[at]
        out_ref[:, which, lanes : lags - 1] = late[at]
        out_ref[:, which, lags - 1 :] = last[at]


def in_vmem():
    return pl.BlockSpec(memory_space=pltpu.VMEM)


def in_smem():
    return pl.BlockSpec(memory_space=pltpu.SMEM)


def on_device(record, alive_mask, owners):
    w_dev, sta_dev, samples = record.shape
    half_len = samples // 2
    sources = OWNERS * sta_dev
    forward = jnp.asarray(forward_table(samples, half_len))
    lag_rows, last_row = map(jnp.asarray, lag_table(samples, half_len, MAXLAG))
    day_count, sta_count = lax.axis_size("day"), lax.axis_size("sta")
    day_pos, sta_pos = lax.axis_index("day"), lax.axis_index("sta")
    src_dev = sources // day_count
    rows = src_dev * sta_dev
    place = jnp.stack([day_pos, sta_pos]).astype(jnp.int32)

    blocks = jnp.broadcast_to(record[None], (sta_count // GROUP,) + record.shape)
    tiles = blocks.reshape(sta_count // GROUP, w_dev, sta_dev, sta_count // w_dev, -1)
    tiles = tiles.transpose(0, 1, 3, 2, 4).reshape(sta_count, sta_count // GROUP, sta_dev, -1)
    everyone = lax.all_to_all(tiles, "sta", 0, 0)

    masks, scale = pl.pallas_call(
        mask_kernel,
        out_shape=[
            jax.ShapeDtypeStruct((w_dev * (sources + sta_dev), 128), jnp.float32),
            jax.ShapeDtypeStruct((2 * rows, 128), jnp.float32),
        ],
        in_specs=[in_smem(), in_smem(), in_vmem()],
        out_specs=[in_vmem()] * 2,
        compiler_params=pltpu.CompilerParams(vmem_limit_bytes=16 * 2**20),
        cost_estimate=pl.CostEstimate(
            flops=2000000000, bytes_accessed=2097152, transcendentals=0
        ),
        name="masks",
    )(place, owners, alive_mask)
    everyone, masks, scale = lax.optimization_barrier((everyone, masks, scale))
    copies = pl.pallas_call(
        pick_kernel,
        out_shape=jax.ShapeDtypeStruct((GROUP, SOURCES * sta_count // GROUP, tiles.shape[3]), record.dtype),
        in_specs=[in_smem(), in_vmem()],
        out_specs=in_vmem(),
        compiler_params=pltpu.CompilerParams(vmem_limit_bytes=8 * 2**20),
        name="pick_owners",
    )(owners, everyone)
    groups = [list(range(first, first + GROUP)) for first in range(0, sta_count, GROUP)]
    gathered = lax.all_to_all(copies, "sta", 0, 0, axis_index_groups=groups)

    pieces = pl.pallas_call(
        cross_kernel,
        out_shape=jax.ShapeDtypeStruct((day_count, 2 * rows + 8, 128), jnp.bfloat16),
        in_specs=[in_vmem()] * 6,
        out_specs=in_vmem(),
        scratch_shapes=[pltpu.VMEM((w_dev * (sources + sta_dev), half_len), jnp.float32)] * 2,
        compiler_params=pltpu.CompilerParams(vmem_limit_bytes=24 * 2**20),
        name="cross_lags",
    )(
        record.reshape(w_dev * sta_dev, samples),
        gathered.reshape(sta_count * sources, -1),
        masks,
        forward,
        lag_rows,
        last_row,
    )
    parts = lax.all_to_all(pieces, "day", 0, 0)
    return pl.pallas_call(
        final_kernel,
        out_shape=jax.ShapeDtypeStruct((sta_dev, src_dev, 2 * MAXLAG + 1), jnp.float32),
        in_specs=[in_vmem()] * 2,
        out_specs=in_vmem(),
        compiler_params=pltpu.CompilerParams(vmem_limit_bytes=16 * 2**20),
        name="sum_parts",
    )(parts, scale)


def solution(mesh):
    return jax.shard_map(
        on_device,
        mesh=mesh,
        in_specs=(P("day", "sta", None), P(), P()),
        out_specs=P("sta", "day", None),
        check_vma=False,
    )
```

```python
import math

import jax
import jax.numpy as jnp
import numpy as np
from jax import lax
from jax.experimental import pallas as pl
from jax.experimental.pallas import tpu as pltpu
from jax.sharding import PartitionSpec as P

MAXLAG = 128
OWNERS = 4
SHARE = 4
SOURCES = 32
GROUP = 8


def forward_table(samples, half_len):
    times = np.arange(samples)[:, None]
    bins = np.arange(1, half_len + 1)[None, :]
    phase = (times * bins % samples).astype(np.float32) * np.float32(2.0 * math.pi / samples)
    return np.concatenate([np.cos(phase), -np.sin(phase)], axis=1).astype(jnp.bfloat16)


def lag_table(samples, half_len, reach):
    bins = np.arange(1, half_len + 1)[:, None]
    shifts = np.arange(-reach, reach + 1)[None, :]
    phase = (bins * shifts % samples).astype(np.float32) * np.float32(2.0 * math.pi / samples)
    weight = (np.where(bins == half_len, 1.0, 2.0) / math.sqrt(samples)).astype(np.float32)
    table = np.concatenate([weight * np.cos(phase), -weight * np.sin(phase)], axis=0)
    table = table.astype(jnp.bfloat16)
    return table[:, :-1], np.pad(table[:, -1:].T, ((0, 15), (0, 0)))


def owner_columns(owners_ref, source, width):
    block = source // width
    owner = jnp.zeros_like(source)
    for which in range(OWNERS):
        owner = jnp.where(block == which, owners_ref[which], owner)
    return owner * width + lax.rem(source, width)


def pick_rows(columns, mask_ref):
    stations = lax.broadcasted_iota(jnp.int32, columns.shape, 1)
    chosen = jnp.where(stations == columns, 1.0, 0.0).astype(jnp.bfloat16)
    mask = mask_ref[...].astype(jnp.float32).astype(jnp.bfloat16)
    return lax.dot_general(
        chosen, mask, (((1,), (1,)), ((), ())), preferred_element_type=jnp.float32
    )


def whiten(rows, forward_ref, masks):
    half_len = forward_ref.shape[1] // 2
    spectrum = jnp.dot(rows, forward_ref[...], preferred_element_type=jnp.float32)
    real_part = spectrum[:, :half_len]
    imag_part = spectrum[:, half_len:]
    magnitude = jnp.sqrt(real_part * real_part + imag_part * imag_part)
    level = jnp.mean(magnitude, axis=-1, keepdims=True)
    factor = masks / (magnitude + 0.3 * level + 1e-06)
    return (
        (real_part * factor).astype(jnp.bfloat16).astype(jnp.float32),
        (imag_part * factor).astype(jnp.bfloat16).astype(jnp.float32),
    )


def mask_columns(place_ref, owners_ref, mask_ref, rows, lanes):
    day_pos, sta_pos = place_ref[0], place_ref[1]
    stations = mask_ref.shape[1]
    sources = SOURCES
    width = sources // OWNERS
    src_dev = rows // width
    first_window = day_pos * SHARE
    row = lax.broadcasted_iota(jnp.int32, (sources + 2 * rows, stations), 0)
    last = row - sources - rows
    columns = jnp.where(
        row < sources,
        owner_columns(owners_ref, row, width),
        jnp.where(
            last < 0,
            sta_pos * width + lax.rem(row - sources, width),
            owner_columns(owners_ref, day_pos * src_dev + last // width, width),
        ),
    )
    alive = pick_rows(columns, mask_ref)
    window = lax.broadcasted_iota(jnp.int32, alive.shape, 1)
    now = [
        jnp.sum(jnp.where(window == first_window + w, alive, 0.0), axis=1, keepdims=True)
        for w in range(SHARE)
    ]
    column = jnp.concatenate(
        [m[:sources] for m in now] + [m[sources : sources + width] for m in now], axis=0
    )
    counts = jnp.sum(
        alive[sources : sources + rows] * alive[sources + rows :], axis=1, keepdims=True
    )
    scale = jnp.broadcast_to(1.0 / jnp.sqrt(jnp.maximum(counts, 1.0)), (rows, lanes))
    lane = lax.broadcasted_iota(jnp.int32, scale.shape, 1)
    arrives = lax.rem(day_pos * rows, lanes) + lax.broadcasted_iota(jnp.int32, scale.shape, 0)
    return column, jnp.concatenate([scale, jnp.where(lane == arrives, scale, 0.0)], axis=0)


def spread_kernel(record_ref, out_ref):
    for copy in range(out_ref.shape[0]):
        out_ref[copy] = record_ref[...]


def pick_kernel(
    place_ref, owners_ref, tiles_ref, mask_ref, out_ref, masks_ref, scale_ref
):
    column, scale_ref[...] = mask_columns(
        place_ref, owners_ref, mask_ref, scale_ref.shape[0] // 2, scale_ref.shape[1]
    )
    masks_ref[...] = jnp.broadcast_to(column, masks_ref.shape)
    picked = jnp.concatenate(
        [
            tiles_ref[owners_ref[which], part]
            for part in range(tiles_ref.shape[1])
            for which in range(OWNERS)
        ],
        axis=0,
    )
    for copy in range(out_ref.shape[0]):
        out_ref[copy] = picked


def cross_kernel(
    own_ref, tiles_ref, masks_ref, forward_ref, lag_ref, last_ref, out_ref, white_re, white_im
):
    width = own_ref.shape[0] // SHARE
    sources = masks_ref.shape[0] // SHARE - width
    half_len = white_re.shape[1]
    tiles = tiles_ref.shape[0] // sources
    wide = tiles // SHARE
    rows = []
    for w in range(SHARE):
        rows.append(
            jnp.concatenate(
                [
                    tiles_ref[t * sources : (t + 1) * sources, :]
                    for t in range(w * wide, (w + 1) * wide)
                ],
                axis=1,
            )
        )
    rows.append(own_ref[...])
    white_re[...], white_im[...] = whiten(
        jnp.concatenate(rows, axis=0), forward_ref, masks_ref[:, 0:1]
    )
    first_own = SHARE * sources
    crossed = []
    for source in range(sources):
        real_sum = jnp.zeros((width, half_len), jnp.float32)
        imag_sum = jnp.zeros((width, half_len), jnp.float32)
        for w in range(SHARE):
            at = w * sources + source
            re, im = white_re[at : at + 1, :], white_im[at : at + 1, :]
            mine = slice(first_own + w * width, first_own + (w + 1) * width)
            mine_re, mine_im = white_re[mine, :], white_im[mine, :]
            real_sum = real_sum + (mine_re * re + mine_im * im)
            imag_sum = imag_sum + (mine_im * re - mine_re * im)
        crossed.append(jnp.concatenate([real_sum, imag_sum], axis=1))
    lanes = out_ref.shape[2]
    piece = sources * width // out_ref.shape[0]
    step = lanes // width
    for first in range(0, sources, step):
        block = jnp.concatenate(crossed[first : first + step], axis=0).astype(jnp.bfloat16)
        lags = jnp.dot(block, lag_ref[...], preferred_element_type=jnp.float32)
        last = lax.dot_general(
            last_ref[...], block, (((1,), (1,)), ((), ())), preferred_element_type=jnp.float32
        )
        for at in range(0, lanes, piece):
            out_ref[(first * width + at) // piece] = jnp.concatenate(
                [lags[at : at + piece, :lanes], lags[at : at + piece, lanes:], last[:8]], axis=0
            ).astype(out_ref.dtype)


def final_kernel(parts_ref, scale_ref, out_ref):
    width, src_dev, lags = out_ref.shape
    rows = width * src_dev
    lanes = parts_ref.shape[2]
    total = parts_ref[0].astype(jnp.float32)
    for part in range(1, parts_ref.shape[0]):
        total = total + parts_ref[part].astype(jnp.float32)
    scale = scale_ref[:rows]
    early = total[:rows] * scale
    late = total[rows : 2 * rows] * scale
    last = jnp.sum(total[2 * rows : 2 * rows + 1] * scale_ref[rows:], axis=1, keepdims=True)
    for which in range(src_dev):
        at = slice(which * width, (which + 1) * width)
        out_ref[:, which, :lanes] = early[at]
        out_ref[:, which, lanes : lags - 1] = late[at]
        out_ref[:, which, lags - 1 :] = last[at]


def in_vmem():
    return pl.BlockSpec(memory_space=pltpu.VMEM)


def in_smem():
    return pl.BlockSpec(memory_space=pltpu.SMEM)


def on_device(record, alive_mask, owners):
    w_dev, sta_dev, samples = record.shape
    half_len = samples // 2
    sources = OWNERS * sta_dev
    forward = jnp.asarray(forward_table(samples, half_len))
    lag_rows, last_row = map(jnp.asarray, lag_table(samples, half_len, MAXLAG))
    day_count, sta_count = lax.axis_size("day"), lax.axis_size("sta")
    day_pos, sta_pos = lax.axis_index("day"), lax.axis_index("sta")
    src_dev = sources // day_count
    rows = src_dev * sta_dev
    place = jnp.stack([day_pos, sta_pos]).astype(jnp.int32)

    record, place = lax.optimization_barrier((record, place))
    blocks = pl.pallas_call(
        spread_kernel,
        out_shape=jax.ShapeDtypeStruct((sta_count // GROUP,) + record.shape, record.dtype),
        in_specs=[in_vmem()],
        out_specs=in_vmem(),
        compiler_params=pltpu.CompilerParams(vmem_limit_bytes=8 * 2**20),
        cost_estimate=pl.CostEstimate(
            flops=4 * 10**9, bytes_accessed=2**19, transcendentals=0
        ),
        name="spread",
    )(record)
    tiles = blocks.reshape(sta_count // GROUP, w_dev, sta_dev, sta_count // w_dev, -1)
    tiles = tiles.transpose(0, 1, 3, 2, 4).reshape(sta_count, sta_count // GROUP, sta_dev, -1)
    everyone = lax.all_to_all(tiles, "sta", 0, 0)

    copies, masks, scale = pl.pallas_call(
        pick_kernel,
        out_shape=[
            jax.ShapeDtypeStruct(
                (GROUP, SOURCES * sta_count // GROUP, tiles.shape[3]), record.dtype
            ),
            jax.ShapeDtypeStruct((w_dev * (sources + sta_dev), 128), jnp.float32),
            jax.ShapeDtypeStruct((2 * rows, 128), jnp.float32),
        ],
        in_specs=[in_smem(), in_smem()] + [in_vmem()] * 2,
        out_specs=[in_vmem()] * 3,
        compiler_params=pltpu.CompilerParams(vmem_limit_bytes=8 * 2**20),
        cost_estimate=pl.CostEstimate(
            flops=4 * 10**9, bytes_accessed=2**19, transcendentals=0
        ),
        name="pick_owners",
    )(place, owners, everyone, alive_mask)
    groups = [list(range(first, first + GROUP)) for first in range(0, sta_count, GROUP)]
    gathered = lax.all_to_all(copies, "sta", 0, 0, axis_index_groups=groups)

    pieces = pl.pallas_call(
        cross_kernel,
        out_shape=jax.ShapeDtypeStruct((day_count, 2 * rows + 8, 128), jnp.bfloat16),
        in_specs=[in_vmem()] * 6,
        out_specs=in_vmem(),
        scratch_shapes=[pltpu.VMEM((w_dev * (sources + sta_dev), half_len), jnp.float32)] * 2,
        compiler_params=pltpu.CompilerParams(vmem_limit_bytes=24 * 2**20),
        name="cross_lags",
    )(
        record.reshape(w_dev * sta_dev, samples),
        gathered.reshape(sta_count * sources, -1),
        masks,
        forward,
        lag_rows,
        last_row,
    )
    parts = lax.all_to_all(pieces, "day", 0, 0)
    return pl.pallas_call(
        final_kernel,
        out_shape=jax.ShapeDtypeStruct((sta_dev, src_dev, 2 * MAXLAG + 1), jnp.float32),
        in_specs=[in_vmem()] * 2,
        out_specs=in_vmem(),
        compiler_params=pltpu.CompilerParams(vmem_limit_bytes=16 * 2**20),
        name="sum_parts",
    )(parts, scale)


def solution(mesh):
    return jax.shard_map(
        on_device,
        mesh=mesh,
        in_specs=(P("day", "sta", None), P(), P()),
        out_specs=P("sta", "day", None),
        check_vma=False,
    )
```

```python
import math

import jax
import jax.numpy as jnp
import numpy as np
from jax import lax
from jax.experimental import pallas as pl
from jax.experimental.pallas import tpu as pltpu
from jax.sharding import PartitionSpec as P

MAXLAG = 128
OWNERS = 4
SHARE = 4
SOURCES = 32
GROUP = 8
SLOTS = 3


def forward_table(samples, half_len):
    times = np.arange(samples)[:, None]
    bins = np.arange(1, half_len + 1)[None, :]
    phase = (times * bins % samples).astype(np.float32) * np.float32(2.0 * math.pi / samples)
    return np.concatenate([np.cos(phase), -np.sin(phase)], axis=1).astype(jnp.bfloat16)


def lag_table(samples, half_len, reach):
    bins = np.arange(1, half_len + 1)[:, None]
    shifts = np.arange(-reach, reach + 1)[None, :]
    phase = (bins * shifts % samples).astype(np.float32) * np.float32(2.0 * math.pi / samples)
    weight = (np.where(bins == half_len, 1.0, 2.0) / math.sqrt(samples)).astype(np.float32)
    table = np.concatenate([weight * np.cos(phase), -weight * np.sin(phase)], axis=0)
    table = table.astype(jnp.bfloat16)
    return table[:, :-1], np.pad(table[:, -1:].T, ((0, 15), (0, 0)))


def owner_columns(owners_ref, source, width):
    block = source // width
    owner = jnp.zeros_like(source)
    for which in range(OWNERS):
        owner = jnp.where(block == which, owners_ref[which], owner)
    return owner * width + lax.rem(source, width)


def pick_rows(columns, mask_ref):
    stations = lax.broadcasted_iota(jnp.int32, columns.shape, 1)
    chosen = jnp.where(stations == columns, 1.0, 0.0).astype(jnp.bfloat16)
    mask = mask_ref[...].astype(jnp.float32).astype(jnp.bfloat16)
    return lax.dot_general(
        chosen, mask, (((1,), (1,)), ((), ())), preferred_element_type=jnp.float32
    )


def whiten(rows, forward_ref, masks):
    half_len = forward_ref.shape[1] // 2
    spectrum = jnp.dot(rows, forward_ref[...], preferred_element_type=jnp.float32)
    real_part = spectrum[:, :half_len]
    imag_part = spectrum[:, half_len:]
    magnitude = jnp.sqrt(real_part * real_part + imag_part * imag_part)
    level = jnp.mean(magnitude, axis=-1, keepdims=True)
    factor = masks / (magnitude + 0.3 * level + 1e-06)
    return (
        (real_part * factor).astype(jnp.bfloat16).astype(jnp.float32),
        (imag_part * factor).astype(jnp.bfloat16).astype(jnp.float32),
    )


def mask_columns(place_ref, owners_ref, mask_ref, rows, lanes):
    day_pos, sta_pos = place_ref[0], place_ref[1]
    stations = mask_ref.shape[1]
    sources = SOURCES
    width = sources // OWNERS
    src_dev = rows // width
    first_window = day_pos * SHARE
    row = lax.broadcasted_iota(jnp.int32, (sources + 2 * rows, stations), 0)
    last = row - sources - rows
    columns = jnp.where(
        row < sources,
        owner_columns(owners_ref, row, width),
        jnp.where(
            last < 0,
            sta_pos * width + lax.rem(row - sources, width),
            owner_columns(owners_ref, day_pos * src_dev + last // width, width),
        ),
    )
    alive = pick_rows(columns, mask_ref)
    window = lax.broadcasted_iota(jnp.int32, alive.shape, 1)
    now = [
        jnp.sum(jnp.where(window == first_window + w, alive, 0.0), axis=1, keepdims=True)
        for w in range(SHARE)
    ]
    column = jnp.concatenate(
        [m[:sources] for m in now] + [m[sources : sources + width] for m in now], axis=0
    )
    counts = jnp.sum(
        alive[sources : sources + rows] * alive[sources + rows :], axis=1, keepdims=True
    )
    scale = jnp.broadcast_to(1.0 / jnp.sqrt(jnp.maximum(counts, 1.0)), (rows, lanes))
    lane = lax.broadcasted_iota(jnp.int32, scale.shape, 1)
    arrives = lax.rem(day_pos * rows, lanes) + lax.broadcasted_iota(jnp.int32, scale.shape, 0)
    return column, jnp.concatenate([scale, jnp.where(lane == arrives, scale, 0.0)], axis=0)


def spread_kernel(record_ref, out_ref):
    for copy in range(out_ref.shape[0]):
        out_ref[copy] = record_ref[...]


def plane_of(sta):
    return lax.rem(lax.div(sta, 2), 2)


def slots_of(owners_ref):
    planes = [plane_of(owners_ref[which]) for which in range(OWNERS)]
    places = []
    for which in range(OWNERS):
        place = jnp.int32(0)
        for other in range(which):
            place = place + jnp.where(planes[other] == planes[which], 1, 0)
        places.append(place)
    return planes, places


def pick_kernel(
    place_ref, owners_ref, tiles_ref, mask_ref, out_ref, masks_ref, scale_ref
):
    column, scale_ref[...] = mask_columns(
        place_ref, owners_ref, mask_ref, scale_ref.shape[0] // 2, scale_ref.shape[1]
    )
    masks_ref[...] = jnp.broadcast_to(column, masks_ref.shape)
    mine = plane_of(place_ref[1])
    planes, places = slots_of(owners_ref)
    parts = tiles_ref.shape[1]
    for slot in range(SLOTS):
        sender = jnp.int32(0)
        for which in range(OWNERS):
            owner = owners_ref[which]
            chosen = jnp.logical_and(planes[which] == mine, places[which] == slot)
            sender = jnp.where(chosen, lax.div(owner, 4) * 2 + lax.rem(owner, 2), sender)
        for part in range(parts):
            tile = tiles_ref[sender, part]
            for copy in range(out_ref.shape[0]):
                out_ref[copy, slot * parts + part] = tile


def cross_kernel(
    owners_ref, own_ref, tiles_ref, masks_ref, forward_ref, lag_ref, last_ref, out_ref, white_re, white_im
):
    width = own_ref.shape[0] // SHARE
    sources = masks_ref.shape[0] // SHARE - width
    half_len = white_re.shape[1]
    planes, places = slots_of(owners_ref)
    wide = tiles_ref.shape[0] // (GROUP * SLOTS)
    rows = []
    for w in range(SHARE):
        device = w // 2 * 4 + w % 2
        starts = [
            ((device + 2 * plane) * SLOTS + place) * wide for plane, place in zip(planes, places)
        ]
        rows.append(
            jnp.concatenate(
                [
                    jnp.concatenate([tiles_ref[start + k] for k in range(wide)], axis=1)
                    for start in starts
                ],
                axis=0,
            )
        )
    rows.append(own_ref[...])
    white_re[...], white_im[...] = whiten(
        jnp.concatenate(rows, axis=0), forward_ref, masks_ref[:, 0:1]
    )
    first_own = SHARE * sources
    crossed = []
    for source in range(sources):
        real_sum = jnp.zeros((width, half_len), jnp.float32)
        imag_sum = jnp.zeros((width, half_len), jnp.float32)
        for w in range(SHARE):
            at = w * sources + source
            re, im = white_re[at : at + 1, :], white_im[at : at + 1, :]
            mine = slice(first_own + w * width, first_own + (w + 1) * width)
            mine_re, mine_im = white_re[mine, :], white_im[mine, :]
            real_sum = real_sum + (mine_re * re + mine_im * im)
            imag_sum = imag_sum + (mine_im * re - mine_re * im)
        crossed.append(jnp.concatenate([real_sum, imag_sum], axis=1))
    lanes = out_ref.shape[2]
    piece = sources * width // out_ref.shape[0]
    step = lanes // width
    for first in range(0, sources, step):
        block = jnp.concatenate(crossed[first : first + step], axis=0).astype(jnp.bfloat16)
        lags = jnp.dot(block, lag_ref[...], preferred_element_type=jnp.float32)
        last = lax.dot_general(
            last_ref[...], block, (((1,), (1,)), ((), ())), preferred_element_type=jnp.float32
        )
        for at in range(0, lanes, piece):
            out_ref[(first * width + at) // piece] = jnp.concatenate(
                [lags[at : at + piece, :lanes], lags[at : at + piece, lanes:], last[:8]], axis=0
            ).astype(out_ref.dtype)


def final_kernel(parts_ref, scale_ref, out_ref):
    width, src_dev, lags = out_ref.shape
    rows = width * src_dev
    lanes = parts_ref.shape[2]
    total = parts_ref[0].astype(jnp.float32)
    for part in range(1, parts_ref.shape[0]):
        total = total + parts_ref[part].astype(jnp.float32)
    scale = scale_ref[:rows]
    early = total[:rows] * scale
    late = total[rows : 2 * rows] * scale
    last = jnp.sum(total[2 * rows : 2 * rows + 1] * scale_ref[rows:], axis=1, keepdims=True)
    for which in range(src_dev):
        at = slice(which * width, (which + 1) * width)
        out_ref[:, which, :lanes] = early[at]
        out_ref[:, which, lanes : lags - 1] = late[at]
        out_ref[:, which, lags - 1 :] = last[at]


def in_vmem():
    return pl.BlockSpec(memory_space=pltpu.VMEM)


def in_smem():
    return pl.BlockSpec(memory_space=pltpu.SMEM)


def on_device(record, alive_mask, owners):
    w_dev, sta_dev, samples = record.shape
    half_len = samples // 2
    sources = OWNERS * sta_dev
    forward = jnp.asarray(forward_table(samples, half_len))
    lag_rows, last_row = map(jnp.asarray, lag_table(samples, half_len, MAXLAG))
    day_count, sta_count = lax.axis_size("day"), lax.axis_size("sta")
    day_pos, sta_pos = lax.axis_index("day"), lax.axis_index("sta")
    src_dev = sources // day_count
    rows = src_dev * sta_dev
    place = jnp.stack([day_pos, sta_pos]).astype(jnp.int32)

    record, place = lax.optimization_barrier((record, place))
    blocks = pl.pallas_call(
        spread_kernel,
        out_shape=jax.ShapeDtypeStruct((sta_count // GROUP,) + record.shape, record.dtype),
        in_specs=[in_vmem()],
        out_specs=in_vmem(),
        compiler_params=pltpu.CompilerParams(vmem_limit_bytes=8 * 2**20),
        cost_estimate=pl.CostEstimate(
            flops=4 * 10**9, bytes_accessed=2**19, transcendentals=0
        ),
        name="spread",
    )(record)
    wide = sta_count // w_dev
    tiles = blocks.reshape(sta_count // GROUP, w_dev, sta_dev, wide, -1)
    tiles = tiles.transpose(0, 1, 3, 2, 4).reshape(sta_count // 2, wide, sta_dev, -1)
    planes = [
        [4 * y + 2 * far + core for y in range(sta_count // 4) for core in range(2)]
        for far in range(2)
    ]
    everyone = lax.all_to_all(tiles, "sta", 0, 0, axis_index_groups=planes)

    copies, masks, scale = pl.pallas_call(
        pick_kernel,
        out_shape=[
            jax.ShapeDtypeStruct((GROUP, SLOTS * wide) + tiles.shape[2:], record.dtype),
            jax.ShapeDtypeStruct((w_dev * (sources + sta_dev), 128), jnp.float32),
            jax.ShapeDtypeStruct((2 * rows, 128), jnp.float32),
        ],
        in_specs=[in_smem(), in_smem()] + [in_vmem()] * 2,
        out_specs=[in_vmem()] * 3,
        compiler_params=pltpu.CompilerParams(vmem_limit_bytes=8 * 2**20),
        cost_estimate=pl.CostEstimate(
            flops=4 * 10**9, bytes_accessed=2**19, transcendentals=0
        ),
        name="pick_owners",
    )(place, owners, everyone, alive_mask)
    groups = [list(range(first, first + GROUP)) for first in range(0, sta_count, GROUP)]
    gathered = lax.all_to_all(copies, "sta", 0, 0, axis_index_groups=groups)

    pieces = pl.pallas_call(
        cross_kernel,
        out_shape=jax.ShapeDtypeStruct((day_count, 2 * rows + 8, 128), jnp.bfloat16),
        in_specs=[in_smem()] + [in_vmem()] * 6,
        out_specs=in_vmem(),
        scratch_shapes=[pltpu.VMEM((w_dev * (sources + sta_dev), half_len), jnp.float32)] * 2,
        compiler_params=pltpu.CompilerParams(vmem_limit_bytes=24 * 2**20),
        name="cross_lags",
    )(
        owners,
        record.reshape(w_dev * sta_dev, samples),
        gathered.reshape((-1,) + tiles.shape[2:]),
        masks,
        forward,
        lag_rows,
        last_row,
    )
    parts = lax.all_to_all(pieces, "day", 0, 0)
    return pl.pallas_call(
        final_kernel,
        out_shape=jax.ShapeDtypeStruct((sta_dev, src_dev, 2 * MAXLAG + 1), jnp.float32),
        in_specs=[in_vmem()] * 2,
        out_specs=in_vmem(),
        compiler_params=pltpu.CompilerParams(vmem_limit_bytes=16 * 2**20),
        name="sum_parts",
    )(parts, scale)


def solution(mesh):
    return jax.shard_map(
        on_device,
        mesh=mesh,
        in_specs=(P("day", "sta", None), P(), P()),
        out_specs=P("sta", "day", None),
        check_vma=False,
    )
```

```python
import math

import jax
import jax.numpy as jnp
import numpy as np
from jax import lax
from jax.experimental import pallas as pl
from jax.experimental.pallas import tpu as pltpu
from jax.sharding import PartitionSpec as P

MAXLAG = 128
OWNERS = 4
SHARE = 4
SOURCES = 32
GROUP = 8
SLOTS = 3


def forward_table(samples, half_len):
    times = np.arange(samples)[:, None]
    bins = np.arange(1, half_len + 1)[None, :]
    phase = (times * bins % samples).astype(np.float32) * np.float32(2.0 * math.pi / samples)
    return np.concatenate([np.cos(phase), -np.sin(phase)], axis=1).astype(jnp.bfloat16)


def lag_table(samples, half_len, reach):
    bins = np.arange(1, half_len + 1)[:, None]
    shifts = np.arange(-reach, reach + 1)[None, :]
    phase = (bins * shifts % samples).astype(np.float32) * np.float32(2.0 * math.pi / samples)
    weight = (np.where(bins == half_len, 1.0, 2.0) / math.sqrt(samples)).astype(np.float32)
    table = np.concatenate([weight * np.cos(phase), -weight * np.sin(phase)], axis=0)
    table = table.astype(jnp.bfloat16)
    return table[:, :-1], np.pad(table[:, -1:].T, ((0, 15), (0, 0)))


def owner_columns(owners_ref, source, width):
    block = source // width
    owner = jnp.zeros_like(source)
    for which in range(OWNERS):
        owner = jnp.where(block == which, owners_ref[which], owner)
    return owner * width + lax.rem(source, width)


def pick_rows(columns, mask_ref):
    stations = lax.broadcasted_iota(jnp.int32, columns.shape, 1)
    chosen = jnp.where(stations == columns, 1.0, 0.0).astype(jnp.bfloat16)
    mask = mask_ref[...].astype(jnp.float32).astype(jnp.bfloat16)
    return lax.dot_general(
        chosen, mask, (((1,), (1,)), ((), ())), preferred_element_type=jnp.float32
    )


def whiten(rows, forward_ref, masks):
    half_len = forward_ref.shape[1] // 2
    spectrum = jnp.dot(rows, forward_ref[...], preferred_element_type=jnp.float32)
    real_part = spectrum[:, :half_len]
    imag_part = spectrum[:, half_len:]
    magnitude = jnp.sqrt(real_part * real_part + imag_part * imag_part)
    level = jnp.mean(magnitude, axis=-1, keepdims=True)
    factor = masks / (magnitude + 0.3 * level + 1e-06)
    return (
        (real_part * factor).astype(jnp.bfloat16).astype(jnp.float32),
        (imag_part * factor).astype(jnp.bfloat16).astype(jnp.float32),
    )


def mask_columns(place_ref, owners_ref, mask_ref, rows, lanes):
    day_pos, sta_pos = place_ref[0], place_ref[1]
    stations = mask_ref.shape[1]
    sources = SOURCES
    width = sources // OWNERS
    src_dev = rows // width
    first_window = day_pos * SHARE
    row = lax.broadcasted_iota(jnp.int32, (sources + 2 * rows, stations), 0)
    last = row - sources - rows
    columns = jnp.where(
        row < sources,
        owner_columns(owners_ref, row, width),
        jnp.where(
            last < 0,
            sta_pos * width + lax.rem(row - sources, width),
            owner_columns(owners_ref, day_pos * src_dev + last // width, width),
        ),
    )
    alive = pick_rows(columns, mask_ref)
    window = lax.broadcasted_iota(jnp.int32, alive.shape, 1)
    now = [
        jnp.sum(jnp.where(window == first_window + w, alive, 0.0), axis=1, keepdims=True)
        for w in range(SHARE)
    ]
    column = jnp.concatenate(
        [m[:sources] for m in now] + [m[sources : sources + width] for m in now], axis=0
    )
    counts = jnp.sum(
        alive[sources : sources + rows] * alive[sources + rows :], axis=1, keepdims=True
    )
    scale = jnp.broadcast_to(1.0 / jnp.sqrt(jnp.maximum(counts, 1.0)), (rows, lanes))
    lane = lax.broadcasted_iota(jnp.int32, scale.shape, 1)
    arrives = lax.rem(day_pos * rows, lanes) + lax.broadcasted_iota(jnp.int32, scale.shape, 0)
    return column, jnp.concatenate([scale, jnp.where(lane == arrives, scale, 0.0)], axis=0)


def spread_kernel(record_ref, out_ref):
    for copy in range(out_ref.shape[0]):
        out_ref[copy] = record_ref[...]


def plane_of(sta):
    return lax.rem(lax.div(sta, 2), 2)


def slots_of(owners_ref):
    planes = [plane_of(owners_ref[which]) for which in range(OWNERS)]
    places = []
    for which in range(OWNERS):
        place = jnp.int32(0)
        for other in range(which):
            place = place + jnp.where(planes[other] == planes[which], 1, 0)
        places.append(place)
    return planes, places


def pick_kernel(
    place_ref, owners_ref, tiles_ref, mask_ref, out_ref, masks_ref, scale_ref
):
    column, scale_ref[...] = mask_columns(
        place_ref, owners_ref, mask_ref, scale_ref.shape[0] // 2, scale_ref.shape[1]
    )
    lanes = masks_ref.shape[1]
    row = lax.broadcasted_iota(jnp.int32, (OWNERS * 2 * SLOTS, lanes), 0)
    planes, places = slots_of(owners_ref)
    held = jnp.zeros(row.shape, jnp.float32)
    for which in range(OWNERS):
        at = (2 * which + planes[which]) * SLOTS + places[which]
        held = held + jnp.where(row == at, 1.0, 0.0)
    masks_ref[...] = jnp.concatenate(
        [jnp.broadcast_to(column, (column.shape[0], lanes)), held], axis=0
    )
    mine = plane_of(place_ref[1])
    parts = tiles_ref.shape[1]
    for slot in range(SLOTS):
        sender = jnp.int32(0)
        for which in range(OWNERS):
            owner = owners_ref[which]
            chosen = jnp.logical_and(planes[which] == mine, places[which] == slot)
            sender = jnp.where(chosen, lax.div(owner, 4) * 2 + lax.rem(owner, 2), sender)
        for part in range(parts):
            tile = tiles_ref[sender, part]
            for copy in range(out_ref.shape[0]):
                out_ref[copy, slot * parts + part] = tile


def cross_kernel(
    own_ref, tiles_ref, masks_ref, forward_ref, lag_ref, last_ref, out_ref, white_re, white_im
):
    width = own_ref.shape[0] // SHARE
    sources = SOURCES
    marks = SHARE * (sources + width)
    half_len = white_re.shape[1]
    wide = tiles_ref.shape[0] // (GROUP * SLOTS)
    slots = 2 * SLOTS
    held = [
        [
            jnp.broadcast_to(masks_ref[pl.ds(marks + which * slots + n, 1), :], (width, 128)) > 0
            for n in range(slots)
        ]
        for which in range(OWNERS)
    ]
    rows = []
    for w in range(SHARE):
        device = w // 2 * 4 + w % 2
        blocks = [[] for _ in range(OWNERS)]
        for k in range(wide):
            tiles = [
                tiles_ref[((device + 2 * (n // SLOTS)) * SLOTS + n % SLOTS) * wide + k].astype(
                    jnp.float32
                )
                for n in range(slots)
            ]
            for which in range(OWNERS):
                tile = tiles[0]
                for n in range(1, slots):
                    tile = jnp.where(held[which][n], tiles[n], tile)
                blocks[which].append(tile)
        rows.append(
            jnp.concatenate([jnp.concatenate(b, axis=1) for b in blocks], axis=0).astype(
                own_ref.dtype
            )
        )
    rows.append(own_ref[...])
    white_re[...], white_im[...] = whiten(
        jnp.concatenate(rows, axis=0), forward_ref, masks_ref[0:marks, 0:1]
    )
    first_own = SHARE * sources
    crossed = []
    for source in range(sources):
        real_sum = jnp.zeros((width, half_len), jnp.float32)
        imag_sum = jnp.zeros((width, half_len), jnp.float32)
        for w in range(SHARE):
            at = w * sources + source
            re, im = white_re[at : at + 1, :], white_im[at : at + 1, :]
            mine = slice(first_own + w * width, first_own + (w + 1) * width)
            mine_re, mine_im = white_re[mine, :], white_im[mine, :]
            real_sum = real_sum + (mine_re * re + mine_im * im)
            imag_sum = imag_sum + (mine_im * re - mine_re * im)
        crossed.append(jnp.concatenate([real_sum, imag_sum], axis=1))
    lanes = out_ref.shape[2]
    piece = sources * width // out_ref.shape[0]
    step = lanes // width
    for first in range(0, sources, step):
        block = jnp.concatenate(crossed[first : first + step], axis=0).astype(jnp.bfloat16)
        lags = jnp.dot(block, lag_ref[...], preferred_element_type=jnp.float32)
        last = lax.dot_general(
            last_ref[...], block, (((1,), (1,)), ((), ())), preferred_element_type=jnp.float32
        )
        for at in range(0, lanes, piece):
            out_ref[(first * width + at) // piece] = jnp.concatenate(
                [lags[at : at + piece, :lanes], lags[at : at + piece, lanes:], last[:8]], axis=0
            ).astype(out_ref.dtype)


def final_kernel(parts_ref, scale_ref, out_ref):
    width, src_dev, lags = out_ref.shape
    rows = width * src_dev
    lanes = parts_ref.shape[2]
    total = parts_ref[0].astype(jnp.float32)
    for part in range(1, parts_ref.shape[0]):
        total = total + parts_ref[part].astype(jnp.float32)
    scale = scale_ref[:rows]
    early = total[:rows] * scale
    late = total[rows : 2 * rows] * scale
    last = jnp.sum(total[2 * rows : 2 * rows + 1] * scale_ref[rows:], axis=1, keepdims=True)
    for which in range(src_dev):
        at = slice(which * width, (which + 1) * width)
        out_ref[:, which, :lanes] = early[at]
        out_ref[:, which, lanes : lags - 1] = late[at]
        out_ref[:, which, lags - 1 :] = last[at]


def in_vmem():
    return pl.BlockSpec(memory_space=pltpu.VMEM)


def in_smem():
    return pl.BlockSpec(memory_space=pltpu.SMEM)


def on_device(record, alive_mask, owners):
    w_dev, sta_dev, samples = record.shape
    half_len = samples // 2
    sources = OWNERS * sta_dev
    forward = jnp.asarray(forward_table(samples, half_len))
    lag_rows, last_row = map(jnp.asarray, lag_table(samples, half_len, MAXLAG))
    day_count, sta_count = lax.axis_size("day"), lax.axis_size("sta")
    day_pos, sta_pos = lax.axis_index("day"), lax.axis_index("sta")
    src_dev = sources // day_count
    rows = src_dev * sta_dev
    place = jnp.stack([day_pos, sta_pos]).astype(jnp.int32)

    record, place = lax.optimization_barrier((record, place))
    blocks = pl.pallas_call(
        spread_kernel,
        out_shape=jax.ShapeDtypeStruct((sta_count // GROUP,) + record.shape, record.dtype),
        in_specs=[in_vmem()],
        out_specs=in_vmem(),
        compiler_params=pltpu.CompilerParams(vmem_limit_bytes=8 * 2**20),
        cost_estimate=pl.CostEstimate(
            flops=4 * 10**9, bytes_accessed=2**19, transcendentals=0
        ),
        name="spread",
    )(record)
    wide = sta_count // w_dev
    tiles = blocks.reshape(sta_count // GROUP, w_dev, sta_dev, wide, -1)
    tiles = tiles.transpose(0, 1, 3, 2, 4).reshape(sta_count // 2, wide, sta_dev, -1)
    planes = [
        [4 * y + 2 * far + core for y in range(sta_count // 4) for core in range(2)]
        for far in range(2)
    ]
    everyone = lax.all_to_all(tiles, "sta", 0, 0, axis_index_groups=planes)

    copies, masks, scale = pl.pallas_call(
        pick_kernel,
        out_shape=[
            jax.ShapeDtypeStruct((GROUP, SLOTS * wide) + tiles.shape[2:], record.dtype),
            jax.ShapeDtypeStruct(
                (w_dev * (sources + sta_dev) + OWNERS * 2 * SLOTS, 128), jnp.float32
            ),
            jax.ShapeDtypeStruct((2 * rows, 128), jnp.float32),
        ],
        in_specs=[in_smem(), in_smem()] + [in_vmem()] * 2,
        out_specs=[in_vmem()] * 3,
        compiler_params=pltpu.CompilerParams(vmem_limit_bytes=8 * 2**20),
        cost_estimate=pl.CostEstimate(
            flops=4 * 10**9, bytes_accessed=2**19, transcendentals=0
        ),
        name="pick_owners",
    )(place, owners, everyone, alive_mask)
    groups = [list(range(first, first + GROUP)) for first in range(0, sta_count, GROUP)]
    gathered = lax.all_to_all(copies, "sta", 0, 0, axis_index_groups=groups)

    pieces = pl.pallas_call(
        cross_kernel,
        out_shape=jax.ShapeDtypeStruct((day_count, 2 * rows + 8, 128), jnp.bfloat16),
        in_specs=[in_vmem()] * 6,
        out_specs=in_vmem(),
        scratch_shapes=[pltpu.VMEM((w_dev * (sources + sta_dev), half_len), jnp.float32)] * 2,
        compiler_params=pltpu.CompilerParams(vmem_limit_bytes=24 * 2**20),
        name="cross_lags",
    )(
        record.reshape(w_dev * sta_dev, samples),
        gathered.reshape((-1,) + tiles.shape[2:]),
        masks,
        forward,
        lag_rows,
        last_row,
    )
    parts = lax.all_to_all(pieces, "day", 0, 0)
    return pl.pallas_call(
        final_kernel,
        out_shape=jax.ShapeDtypeStruct((sta_dev, src_dev, 2 * MAXLAG + 1), jnp.float32),
        in_specs=[in_vmem()] * 2,
        out_specs=in_vmem(),
        compiler_params=pltpu.CompilerParams(vmem_limit_bytes=16 * 2**20),
        name="sum_parts",
    )(parts, scale)


def solution(mesh):
    return jax.shard_map(
        on_device,
        mesh=mesh,
        in_specs=(P("day", "sta", None), P(), P()),
        out_specs=P("sta", "day", None),
        check_vma=False,
    )
```

```python
import math

import jax
import jax.numpy as jnp
import numpy as np
from jax import lax
from jax.experimental import pallas as pl
from jax.experimental.pallas import tpu as pltpu
from jax.sharding import PartitionSpec as P

MAXLAG = 128
OWNERS = 4
SHARE = 4
SOURCES = 32
GROUP = 8
SLOTS = 3


def forward_table(samples, half_len):
    times = np.arange(samples)[:, None]
    bins = np.arange(1, half_len + 1)[None, :]
    phase = (times * bins % samples).astype(np.float32) * np.float32(2.0 * math.pi / samples)
    return np.concatenate([np.cos(phase), -np.sin(phase)], axis=1).astype(jnp.bfloat16)


def lag_table(samples, half_len, reach):
    bins = np.arange(1, half_len + 1)[:, None]
    shifts = np.arange(-reach, reach + 1)[None, :]
    phase = (bins * shifts % samples).astype(np.float32) * np.float32(2.0 * math.pi / samples)
    weight = (np.where(bins == half_len, 1.0, 2.0) / math.sqrt(samples)).astype(np.float32)
    table = np.concatenate([weight * np.cos(phase), -weight * np.sin(phase)], axis=0)
    table = table.astype(jnp.bfloat16)
    return table[:, :-1], np.pad(table[:, -1:].T, ((0, 15), (0, 0)))


def owner_columns(owners_ref, source, width):
    block = source // width
    owner = jnp.zeros_like(source)
    for which in range(OWNERS):
        owner = jnp.where(block == which, owners_ref[which], owner)
    return owner * width + lax.rem(source, width)


def pick_rows(columns, mask_ref):
    stations = lax.broadcasted_iota(jnp.int32, columns.shape, 1)
    chosen = jnp.where(stations == columns, 1.0, 0.0).astype(jnp.bfloat16)
    mask = mask_ref[...].astype(jnp.float32).astype(jnp.bfloat16)
    return lax.dot_general(
        chosen, mask, (((1,), (1,)), ((), ())), preferred_element_type=jnp.float32
    )


def whiten(rows, forward_ref, masks):
    half_len = forward_ref.shape[1] // 2
    spectrum = jnp.dot(rows, forward_ref[...], preferred_element_type=jnp.float32)
    real_part = spectrum[:, :half_len]
    imag_part = spectrum[:, half_len:]
    magnitude = jnp.sqrt(real_part * real_part + imag_part * imag_part)
    level = jnp.mean(magnitude, axis=-1, keepdims=True)
    factor = masks / (magnitude + 0.3 * level + 1e-06)
    return (
        (real_part * factor).astype(jnp.bfloat16).astype(jnp.float32),
        (imag_part * factor).astype(jnp.bfloat16).astype(jnp.float32),
    )


def mask_columns(day_pos, sta_pos, owners_ref, mask_ref, rows, lanes):
    stations = mask_ref.shape[1]
    sources = SOURCES
    width = sources // OWNERS
    src_dev = rows // width
    first_window = day_pos * SHARE
    row = lax.broadcasted_iota(jnp.int32, (sources + 2 * rows, stations), 0)
    last = row - sources - rows
    columns = jnp.where(
        row < sources,
        owner_columns(owners_ref, row, width),
        jnp.where(
            last < 0,
            sta_pos * width + lax.rem(row - sources, width),
            owner_columns(owners_ref, day_pos * src_dev + last // width, width),
        ),
    )
    alive = pick_rows(columns, mask_ref)
    window = lax.broadcasted_iota(jnp.int32, alive.shape, 1)
    now = [
        jnp.sum(jnp.where(window == first_window + w, alive, 0.0), axis=1, keepdims=True)
        for w in range(SHARE)
    ]
    column = jnp.concatenate(
        [m[:sources] for m in now] + [m[sources : sources + width] for m in now], axis=0
    )
    counts = jnp.sum(
        alive[sources : sources + rows] * alive[sources + rows :], axis=1, keepdims=True
    )
    scale = jnp.broadcast_to(1.0 / jnp.sqrt(jnp.maximum(counts, 1.0)), (rows, lanes))
    lane = lax.broadcasted_iota(jnp.int32, scale.shape, 1)
    arrives = lax.rem(day_pos * rows, lanes) + lax.broadcasted_iota(jnp.int32, scale.shape, 0)
    return column, jnp.concatenate([scale, jnp.where(lane == arrives, scale, 0.0)], axis=0)


def spread_kernel(record_ref, out_ref):
    for copy in range(out_ref.shape[0]):
        out_ref[copy] = record_ref[...]


def plane_of(sta):
    return lax.rem(lax.div(sta, 2), 2)


def slots_of(owners_ref):
    planes = [plane_of(owners_ref[which]) for which in range(OWNERS)]
    places = []
    for which in range(OWNERS):
        place = jnp.int32(0)
        for other in range(which):
            place = place + jnp.where(planes[other] == planes[which], 1, 0)
        places.append(place)
    return planes, places


def pick_kernel(
    owners_ref, tiles_ref, mask_ref, out_ref, masks_ref, scale_ref
):
    day_pos, sta_pos = lax.axis_index("day"), lax.axis_index("sta")
    column, scale_ref[...] = mask_columns(
        day_pos, sta_pos, owners_ref, mask_ref, scale_ref.shape[0] // 2, scale_ref.shape[1]
    )
    lanes = masks_ref.shape[1]
    row = lax.broadcasted_iota(jnp.int32, (OWNERS * 2 * SLOTS, lanes), 0)
    planes, places = slots_of(owners_ref)
    held = jnp.zeros(row.shape, jnp.float32)
    for which in range(OWNERS):
        at = (2 * which + planes[which]) * SLOTS + places[which]
        held = held + jnp.where(row == at, 1.0, 0.0)
    masks_ref[...] = jnp.concatenate(
        [jnp.broadcast_to(column, (column.shape[0], lanes)), held], axis=0
    )
    mine = plane_of(sta_pos)
    parts = tiles_ref.shape[1]
    for slot in range(SLOTS):
        sender = jnp.int32(0)
        for which in range(OWNERS):
            owner = owners_ref[which]
            chosen = jnp.logical_and(planes[which] == mine, places[which] == slot)
            sender = jnp.where(chosen, lax.div(owner, 4) * 2 + lax.rem(owner, 2), sender)
        for part in range(parts):
            tile = tiles_ref[sender, part]
            for copy in range(out_ref.shape[0]):
                out_ref[copy, slot * parts + part] = tile


def cross_kernel(
    own_ref, tiles_ref, masks_ref, forward_ref, lag_ref, last_ref, out_ref, white_re, white_im
):
    width = own_ref.shape[0] // SHARE
    sources = SOURCES
    marks = SHARE * (sources + width)
    half_len = white_re.shape[1]
    wide = tiles_ref.shape[0] // (GROUP * SLOTS)
    slots = 2 * SLOTS
    held = [
        [
            jnp.broadcast_to(masks_ref[pl.ds(marks + which * slots + n, 1), :], (width, 128)) > 0
            for n in range(slots)
        ]
        for which in range(OWNERS)
    ]
    rows = []
    for w in range(SHARE):
        device = w // 2 * 4 + w % 2
        blocks = [[] for _ in range(OWNERS)]
        for k in range(wide):
            tiles = [
                tiles_ref[((device + 2 * (n // SLOTS)) * SLOTS + n % SLOTS) * wide + k].astype(
                    jnp.float32
                )
                for n in range(slots)
            ]
            for which in range(OWNERS):
                tile = tiles[0]
                for n in range(1, slots):
                    tile = jnp.where(held[which][n], tiles[n], tile)
                blocks[which].append(tile)
        rows.append(
            jnp.concatenate([jnp.concatenate(b, axis=1) for b in blocks], axis=0).astype(
                own_ref.dtype
            )
        )
    rows.append(own_ref[...])
    white_re[...], white_im[...] = whiten(
        jnp.concatenate(rows, axis=0), forward_ref, masks_ref[0:marks, 0:1]
    )
    first_own = SHARE * sources
    crossed = []
    for source in range(sources):
        real_sum = jnp.zeros((width, half_len), jnp.float32)
        imag_sum = jnp.zeros((width, half_len), jnp.float32)
        for w in range(SHARE):
            at = w * sources + source
            re, im = white_re[at : at + 1, :], white_im[at : at + 1, :]
            mine = slice(first_own + w * width, first_own + (w + 1) * width)
            mine_re, mine_im = white_re[mine, :], white_im[mine, :]
            real_sum = real_sum + (mine_re * re + mine_im * im)
            imag_sum = imag_sum + (mine_im * re - mine_re * im)
        crossed.append(jnp.concatenate([real_sum, imag_sum], axis=1))
    lanes = out_ref.shape[2]
    piece = sources * width // out_ref.shape[0]
    step = lanes // width
    for first in range(0, sources, step):
        block = jnp.concatenate(crossed[first : first + step], axis=0).astype(jnp.bfloat16)
        lags = jnp.dot(block, lag_ref[...], preferred_element_type=jnp.float32)
        last = lax.dot_general(
            last_ref[...], block, (((1,), (1,)), ((), ())), preferred_element_type=jnp.float32
        )
        for at in range(0, lanes, piece):
            out_ref[(first * width + at) // piece] = jnp.concatenate(
                [lags[at : at + piece, :lanes], lags[at : at + piece, lanes:], last[:8]], axis=0
            ).astype(out_ref.dtype)


def final_kernel(parts_ref, scale_ref, out_ref):
    width, src_dev, lags = out_ref.shape
    rows = width * src_dev
    lanes = parts_ref.shape[2]
    total = parts_ref[0].astype(jnp.float32)
    for part in range(1, parts_ref.shape[0]):
        total = total + parts_ref[part].astype(jnp.float32)
    scale = scale_ref[:rows]
    early = total[:rows] * scale
    late = total[rows : 2 * rows] * scale
    last = jnp.sum(total[2 * rows : 2 * rows + 1] * scale_ref[rows:], axis=1, keepdims=True)
    for which in range(src_dev):
        at = slice(which * width, (which + 1) * width)
        out_ref[:, which, :lanes] = early[at]
        out_ref[:, which, lanes : lags - 1] = late[at]
        out_ref[:, which, lags - 1 :] = last[at]


def in_vmem():
    return pl.BlockSpec(memory_space=pltpu.VMEM)


def in_smem():
    return pl.BlockSpec(memory_space=pltpu.SMEM)


def on_device(record, alive_mask, owners):
    w_dev, sta_dev, samples = record.shape
    half_len = samples // 2
    sources = OWNERS * sta_dev
    forward = jnp.asarray(forward_table(samples, half_len))
    lag_rows, last_row = map(jnp.asarray, lag_table(samples, half_len, MAXLAG))
    day_count, sta_count = lax.axis_size("day"), lax.axis_size("sta")
    src_dev = sources // day_count
    rows = src_dev * sta_dev

    blocks = pl.pallas_call(
        spread_kernel,
        out_shape=jax.ShapeDtypeStruct((sta_count // GROUP,) + record.shape, record.dtype),
        in_specs=[in_vmem()],
        out_specs=in_vmem(),
        compiler_params=pltpu.CompilerParams(vmem_limit_bytes=8 * 2**20),
        cost_estimate=pl.CostEstimate(
            flops=4 * 10**9, bytes_accessed=2**19, transcendentals=0
        ),
        name="spread",
    )(record)
    wide = sta_count // w_dev
    tiles = blocks.reshape(sta_count // GROUP, w_dev, sta_dev, wide, -1)
    tiles = tiles.transpose(0, 1, 3, 2, 4).reshape(sta_count // 2, wide, sta_dev, -1)
    planes = [
        [4 * y + 2 * far + core for y in range(sta_count // 4) for core in range(2)]
        for far in range(2)
    ]
    everyone = lax.all_to_all(tiles, "sta", 0, 0, axis_index_groups=planes)

    copies, masks, scale = pl.pallas_call(
        pick_kernel,
        out_shape=[
            jax.ShapeDtypeStruct((GROUP, SLOTS * wide) + tiles.shape[2:], record.dtype),
            jax.ShapeDtypeStruct(
                (w_dev * (sources + sta_dev) + OWNERS * 2 * SLOTS, 128), jnp.float32
            ),
            jax.ShapeDtypeStruct((2 * rows, 128), jnp.float32),
        ],
        in_specs=[in_smem()] + [in_vmem()] * 2,
        out_specs=[in_vmem()] * 3,
        compiler_params=pltpu.CompilerParams(vmem_limit_bytes=8 * 2**20),
        cost_estimate=pl.CostEstimate(
            flops=4 * 10**9, bytes_accessed=2**19, transcendentals=0
        ),
        name="pick_owners",
    )(owners, everyone, alive_mask)
    groups = [list(range(first, first + GROUP)) for first in range(0, sta_count, GROUP)]
    gathered = lax.all_to_all(copies, "sta", 0, 0, axis_index_groups=groups)

    pieces = pl.pallas_call(
        cross_kernel,
        out_shape=jax.ShapeDtypeStruct((day_count, 2 * rows + 8, 128), jnp.bfloat16),
        in_specs=[in_vmem()] * 6,
        out_specs=in_vmem(),
        scratch_shapes=[pltpu.VMEM((w_dev * (sources + sta_dev), half_len), jnp.float32)] * 2,
        compiler_params=pltpu.CompilerParams(vmem_limit_bytes=24 * 2**20),
        name="cross_lags",
    )(
        record.reshape(w_dev * sta_dev, samples),
        gathered.reshape((-1,) + tiles.shape[2:]),
        masks,
        forward,
        lag_rows,
        last_row,
    )
    parts = lax.all_to_all(pieces, "day", 0, 0)
    return pl.pallas_call(
        final_kernel,
        out_shape=jax.ShapeDtypeStruct((sta_dev, src_dev, 2 * MAXLAG + 1), jnp.float32),
        in_specs=[in_vmem()] * 2,
        out_specs=in_vmem(),
        compiler_params=pltpu.CompilerParams(vmem_limit_bytes=16 * 2**20),
        name="sum_parts",
    )(parts, scale)


def solution(mesh):
    return jax.shard_map(
        on_device,
        mesh=mesh,
        in_specs=(P("day", "sta", None), P(), P()),
        out_specs=P("sta", "day", None),
        check_vma=False,
    )
```
